512 devices in a mesh: row: 32 (over x_lo, z), col: 16 (over y, x_hi, core).
Axes of the slice: x: 4 (x_hi: 2, x_lo: 2; x = x_hi * 2 + x_lo), y: 4, z: 16, core: 2. Of those that a mesh axis runs over, the one named last changes fastest.
Arguments:
- density: float32 [128, 16, 128, 128], P('row', 'col'), may hold values from -1 to 1
- columns: int32 [128, 16], replicated, may hold values from -1 to 7, as said below
Outputs:
- squared: float32 [128, 16, 128, 128], P('row', 'col')
- purified: float32 [128, 16, 128, 128], P('row', 'col')
The draws below stay inside these ranges and needn't reach their ends.
Inputs may be any that keep to these rules, and one draw needn't show every extreme that they name: Each block row has at most one filled block in each group of 8 block columns; every diagonal block is filled (entry (r, r // 8) is r % 8); the share of filled groups differs from block row to block row.
All inputs are finite; a program needn't handle non-finite values.
Results may differ from the reference program's by a relative error of at most 0.0003.
Values sent between devices are 32-bit elements; how exact they have to be, the bound alone decides.
No kernel may reach another device: no remote copies, remote signals or barrier semaphores. Data moves between devices by JAX's collectives and lax.ppermute only.
A program may use at most 128 MiB of HBM per device.

```python
import jax
import jax.numpy as jnp
from jax import lax

BLK = 128
NB = 128
BW = 8
N_COL = 16


def draw_columns(key, part):
    key = jax.random.fold_in(key, 11)
    level_key, score_key, offset_key = jax.random.split(key, 3)
    levels = jax.random.randint(level_key, (NB, 1), 1, 10)
    scores = jax.random.randint(score_key, (NB, N_COL), 0, 10)
    offsets = jax.random.randint(offset_key, (NB, N_COL), 0, BW)
    rows = jnp.arange(NB, dtype=jnp.int32)[:, None]
    groups = jnp.arange(N_COL, dtype=jnp.int32)[None, :]
    home = groups == rows // BW
    chosen = jnp.where(scores < levels, offsets, -1)
    return jnp.where(home, rows % BW, chosen).astype(jnp.int32)


def draw_density(key, part):
    key = jax.random.fold_in(key, 23)
    first_key = jax.random.fold_in(key, 0)
    sigma = 0.5 / BLK ** 0.5
    values = jnp.clip(jax.random.normal(first_key, (NB, N_COL, BLK, BLK), jnp.float32), -4.0, 4.0)
    rows = jnp.arange(NB, dtype=jnp.int32)[:, None]
    groups = jnp.arange(N_COL, dtype=jnp.int32)[None, :]
    home = (groups == rows // BW).astype(jnp.float32)
    identity = jnp.eye(BLK, dtype=jnp.float32)
    return values * sigma + 0.5 * home[:, :, None, None] * identity[None, None, :, :]


def setup_inputs(seed: int = 0) -> dict:
    streams_of = jax.random.split(jax.random.key(seed), 3)
    return {
        "density": draw_density(jax.random.fold_in(streams_of[2], 71), 0),
        "columns": draw_columns(jax.random.fold_in(streams_of[2], 71), 0),
    }


def reference(density, columns):
    filled = columns >= 0
    groups = jnp.arange(N_COL, dtype=jnp.int32)
    source_rows = (groups[None, :] * BW + jnp.maximum(columns, 0)).astype(jnp.int32)
    keep = filled[:, :, None, None].astype(jnp.float32)
    masked = density * keep

    def product(left_part):
        def one_row(row_number):
            row_cols = columns[row_number]
            row_filled = filled[row_number]
            sources = source_rows[row_number]
            chosen_blocks = masked[sources]
            weights = row_filled[:, None] & (columns[sources] == row_cols[None, :]) & row_filled[None, :]
            scaled = left_part[row_number][:, None, :, :] * weights[:, :, None, None].astype(jnp.float32)
            return jnp.einsum("joab,jobc->oac", scaled, chosen_blocks, precision=lax.Precision.HIGHEST)

        return lax.map(one_row, jnp.arange(NB, dtype=jnp.int32))

    squared = product(masked) * keep
    cubed = product(squared) * keep
    return squared, 3.0 * squared - 2.0 * cubed
```

```python
import functools

import jax
import jax.numpy as jnp
from jax import lax
from jax.experimental import pallas as pl
from jax.experimental.pallas import tpu as pltpu
from jax.sharding import PartitionSpec as P

F32 = jnp.float32
I32 = jnp.int32
VMEM = pl.BlockSpec(memory_space=pltpu.VMEM)
SMEM = pl.BlockSpec(memory_space=pltpu.SMEM)
PARAMS = pltpu.CompilerParams(vmem_limit_bytes=48 << 20)
SIZES = (8, 10, 12, 14, 18, 64)


def iota(shape, dim):
    return lax.broadcasted_iota(I32, shape, dim)


def eq(a, b):
    return (a == b).astype(F32)


def dot(a, b):
    return jnp.dot(a, b, preferred_element_type=F32)


def plan_kernel(rows, row_devs, groups, width, here, cols_ref, colst_ref, right_ref, left_ref, code_ref, info_ref):
    me, g_me = here[0], here[1]
    local = rows // row_devs
    cand = local * groups
    slots = cand
    cols = cols_ref[...]
    colst = colst_ref[...]
    s_j = eq(iota((rows, groups), 0) // width, iota((rows, groups), 1))
    j_s = eq(iota((groups, rows), 1) // width, iota((groups, rows), 0))
    mine_row = jnp.sum(jnp.where(iota((groups, rows), 0) == g_me, colst, 0.0), axis=0, keepdims=True)
    mine_col = jnp.sum(jnp.where(iota((rows, groups), 1) == g_me, cols, 0.0), axis=1, keepdims=True)
    by_source = dot(s_j, colst)
    term = (
        (by_source == (iota((rows, rows), 0) % width).astype(F32))
        & (mine_col == mine_row)
        & (mine_row >= 0)
    ).astype(F32)
    term = dot(j_s, term)
    source = iota((groups, rows), 0).astype(F32) * width + colst
    source = source.astype(I32)
    away = jnp.where((source // local) != (iota((groups, rows), 1) // local), term, 0.0)
    before = (iota((groups, groups), 1) < iota((groups, groups), 0)).astype(F32)
    count = jnp.sum(away, axis=0, keepdims=True)
    r0, r1 = iota((rows, rows), 0), iota((rows, rows), 1)
    earlier = ((r0 // local == r1 // local) & (r0 < r1)).astype(F32)
    rank = dot(before, away) + dot(jnp.broadcast_to(count, (8, rows)), earlier)[:1]
    rank = jnp.where(away > 0, rank, -1.0)
    slot = iota((slots, rows), 0).astype(F32)
    source_f = source.astype(F32)
    found = jnp.zeros((slots, rows), F32)
    for j in range(groups):
        found = found + jnp.where(rank[j : j + 1] == slot, source_f[j : j + 1], 0.0)
    fold = eq(iota((rows, row_devs), 0) // local, iota((rows, row_devs), 1))
    right_ref[...] = dot(found, fold).astype(I32)
    c0 = iota((cand, rows), 0)
    row_val = dot(eq(iota((cand, rows), 1), me * local + c0 // groups), cols)
    c1 = iota((cand, groups), 0)
    g1 = iota((cand, groups), 1)
    own = jnp.sum(jnp.where(g1 == c1 % groups, row_val, 0.0), axis=1, keepdims=True)
    q_1 = iota((cand, 1), 0) // groups
    j_1 = iota((cand, 1), 0) % groups
    s_1 = j_1 * width + own.astype(I32)
    s_val = dot(eq(iota((cand, rows), 1), s_1), cols)
    terms = ((own >= 0) & (row_val >= 0) & (s_val == row_val)).astype(F32)
    lefts = jnp.where(c1 % groups != g1, terms, 0.0)
    lower = (iota((cand, cand), 1) < iota((cand, cand), 0)).astype(F32)
    rank_l = dot(lower, lefts)
    marked = jnp.where(lefts > 0, rank_l, -1.0)
    piece = j_1 * local + q_1
    piece_f = piece.astype(F32)
    slot_g = iota((slots, groups), 0).astype(F32)
    got = jnp.zeros((slots, groups), F32)
    for k in range(cand):
        got = got + jnp.where(marked[k : k + 1] == slot_g, float((k % groups) * local + k // groups), 0.0)
    left_ref[...] = got.astype(I32)
    pick = g1 == g_me
    mine = jnp.sum(jnp.where(pick, terms, 0.0), axis=1, keepdims=True)
    l_rank = jnp.sum(jnp.where(pick, rank_l, 0.0), axis=1, keepdims=True)
    is_away = (s_1 // local != me).astype(F32)
    wide = iota((cand, 128), 1)
    both = jnp.where(wide == 0, mine, jnp.where(wide == 1, mine * is_away, 0.0))
    ranks = dot(lower, both)
    order = jnp.sum(jnp.where(wide == 0, ranks, 0.0), axis=1, keepdims=True)
    r_rank = jnp.sum(jnp.where(wide == 1, ranks, 0.0), axis=1, keepdims=True)
    l_at = jnp.where(j_1 == g_me, slots + q_1, l_rank.astype(I32))
    r_at = jnp.where(is_away > 0, r_rank.astype(I32), slots + s_1 % local)
    code = (q_1 + 4 * piece + 256 * l_at + 32768 * r_at).astype(F32)
    hot = (mine > 0) & (order == wide.astype(F32))
    code_ref[...] = jnp.sum(jnp.where(hot, code, 0.0), axis=0, keepdims=True).astype(I32)
    values = rows // groups
    copy = eq(iota((groups, rows), 1) % groups, iota((groups, rows), 0))
    has = eq(dot(cols, copy), (iota((rows, rows), 1) // groups).astype(F32))
    filled = eq(dot(cols, j_s), (r1 % width).astype(F32))
    far = jnp.where(r0 // local != r1 // local, filled, 0.0)
    group_of = eq(iota((row_devs, rows), 1) // local, iota((row_devs, rows), 0))
    back = eq(iota((rows, groups), 0) % groups, iota((rows, groups), 1))
    need_r = dot(dot(group_of, dot(far, has) * has), back)
    need_l = dot(dot(group_of, (dot(filled, has) - 1.0) * has), back)
    most = jnp.max(jnp.maximum(need_r, need_l), axis=(0, 1), keepdims=True)
    number = jnp.sum(mine, axis=(0, 1), keepdims=True)
    info_ref[...] = jnp.where(iota((1, 128), 1) == 0, number, most).astype(I32)


def pack_kernel(size, table, pieces, out):
    def one(d, _):
        for slot in range(size):
            out[d, slot] = pieces[table[slot, d]]
        return 0

    lax.fori_loop(0, out.shape[0], one, 0)


def halves(block):
    high = block.astype(jnp.bfloat16)
    return high, (block - high.astype(F32)).astype(jnp.bfloat16)


def product(left, right):
    lh, ll = halves(left)
    rh, rl = halves(right)
    return dot(lh, rh) + (dot(lh, rl) + dot(ll, rh))


def square_kernel(size, code, info, x, panel, came, squared, spread, rights):
    rows = came.shape[2]

    def unpack(c, _):
        for h in range(came.shape[0]):
            rights[c, h * rows : (h + 1) * rows, :] = came[h, c]
        return 0

    lax.fori_loop(0, size, unpack, 0)
    local = x.shape[0]
    rights[size : size + local] = x[...]
    squared[...] = jnp.zeros_like(squared)

    def one(t, _):
        word = code[0, t]
        q, piece, r_at = word % 4, (word // 4) % 64, word // 32768
        r_at = jnp.where(r_at >= 64, r_at - 64 + size, r_at)
        squared[q] += product(panel[piece], rights[r_at])
        return 0

    lax.fori_loop(0, info[0, 0], one, 0)
    tall = spread.shape[2]
    for k in range(spread.shape[0]):
        spread[k] = squared[:, k * tall : (k + 1) * tall, :]


def cube_kernel(size, code, info, squared, came, rights, purified, lefts):
    rows = came.shape[2]
    local = squared.shape[0]

    def unpack(c, _):
        for h in range(came.shape[0]):
            lefts[c, h * rows : (h + 1) * rows, :] = came[h, c]
        return 0

    lax.fori_loop(0, size, unpack, 0)
    lefts[size : size + local] = squared[...]
    purified[...] = 3.0 * squared[...]

    def one(t, _):
        word = code[0, t]
        q, l_at, r_at = word % 4, (word // 256) % 128, word // 32768
        l_at = jnp.where(l_at >= 64, l_at - 64 + size, l_at)
        r_at = jnp.where(r_at >= 64, r_at - 64 + size, r_at)
        purified[q] += -2.0 * product(lefts[l_at], rights[r_at])
        return 0

    lax.fori_loop(0, info[0, 0], one, 0)


def shape(*dims, dtype=F32):
    return jax.ShapeDtypeStruct(dims, dtype)


def branch(size, x, right, left, code, info):
    local, order, _ = x.shape
    row_devs = lax.axis_size("row")
    groups = lax.axis_size("col")
    fine, tall = order // row_devs, order // groups
    panel = lax.all_gather(x, "col", axis=0, tiled=True)
    spread = x.reshape(local, row_devs, fine, order).transpose(1, 0, 2, 3)
    held = lax.all_to_all(spread, "row", 0, 0, tiled=True)
    held = held.reshape(row_devs * local, fine, order)
    out = pl.pallas_call(
        functools.partial(pack_kernel, size),
        out_shape=shape(row_devs, size, fine, order),
        in_specs=[SMEM, VMEM],
        out_specs=VMEM,
        compiler_params=PARAMS,
        name="pack_right",
    )(right, held)
    came = lax.all_to_all(out, "row", 0, 0, tiled=True)
    squared, spread, rights = pl.pallas_call(
        functools.partial(square_kernel, size),
        out_shape=(
            shape(local, order, order),
            shape(groups, local, tall, order),
            shape(size + local, order, order),
        ),
        in_specs=[SMEM, SMEM, VMEM, VMEM, VMEM],
        out_specs=(VMEM, VMEM, VMEM),
        compiler_params=PARAMS,
        name="square",
    )(code, info, x, panel, came)
    held = lax.all_to_all(spread, "col", 0, 0, tiled=True)
    held = held.reshape(groups * local, tall, order)
    out = pl.pallas_call(
        functools.partial(pack_kernel, size),
        out_shape=shape(groups, size, tall, order),
        in_specs=[SMEM, VMEM],
        out_specs=VMEM,
        compiler_params=PARAMS,
        name="pack_left",
    )(left, held)
    came = lax.all_to_all(out, "col", 0, 0, tiled=True)
    purified = pl.pallas_call(
        functools.partial(cube_kernel, size),
        out_shape=shape(local, order, order),
        in_specs=[SMEM, SMEM, VMEM, VMEM, VMEM],
        out_specs=VMEM,
        scratch_shapes=[pltpu.VMEM((size + local, order, order), F32)],
        compiler_params=PARAMS,
        name="cube",
    )(code, info, squared, came, rights)
    return squared, purified


def body(density, columns):
    row_devs = lax.axis_size("row")
    rows, groups = columns.shape
    width = rows // groups
    local = density.shape[0]
    cand = local * groups
    here = jnp.stack([lax.axis_index("row"), lax.axis_index("col")]).astype(I32)
    cols = columns.astype(F32)
    right, left, code, info = pl.pallas_call(
        functools.partial(plan_kernel, rows, row_devs, groups, width),
        out_shape=(
            shape(cand, row_devs, dtype=I32),
            shape(cand, groups, dtype=I32),
            shape(1, 128, dtype=I32),
            shape(1, 128, dtype=I32),
        ),
        in_specs=[SMEM, VMEM, VMEM],
        out_specs=(VMEM, VMEM, VMEM, VMEM),
        compiler_params=PARAMS,
        name="plan",
    )(here, cols, cols.T)
    most = info[0, 1]
    which = sum((most > size).astype(I32) for size in SIZES[:-1])
    x = density[:, 0]
    squared, purified = lax.switch(
        which, [functools.partial(branch, size) for size in SIZES], x, right, left, code, info
    )
    return squared[:, None], purified[:, None]


def solution(mesh):
    return jax.shard_map(
        body,
        mesh=mesh,
        in_specs=(P("row", "col", None, None), P()),
        out_specs=(P("row", "col", None, None), P("row", "col", None, None)),
        check_vma=False,
    )
```

```python
import functools

import jax
import jax.numpy as jnp
from jax import lax
from jax.experimental import pallas as pl
from jax.experimental.pallas import tpu as pltpu
from jax.sharding import PartitionSpec as P

F32 = jnp.float32
I32 = jnp.int32
VMEM = pl.BlockSpec(memory_space=pltpu.VMEM)
HBM = pl.BlockSpec(memory_space=pltpu.HBM)
SMEM = pl.BlockSpec(memory_space=pltpu.SMEM)
WIDE = pltpu.CompilerParams(vmem_limit_bytes=57 << 20)
PARAMS = pltpu.CompilerParams(vmem_limit_bytes=24 << 20)
SIZES = (6, 7, 8, 9, 10, 11, 12, 13, 14, 16, 20, 64)


def iota(shape, dim):
    return lax.broadcasted_iota(I32, shape, dim)


def eq(a, b):
    return (a == b).astype(F32)


def dot(a, b):
    return jnp.dot(a, b, preferred_element_type=F32)


def plan_kernel(rows, row_devs, groups, width, here, cols_ref, colst_ref, right_ref, left_ref, code_ref, info_ref):
    me, g_me = here[0], here[1]
    local = rows // row_devs
    cand = local * groups
    slots = cand
    cols = cols_ref[...]
    colst = colst_ref[...]
    s_j = eq(iota((rows, groups), 0) // width, iota((rows, groups), 1))
    j_s = eq(iota((groups, rows), 1) // width, iota((groups, rows), 0))
    mine_row = jnp.sum(jnp.where(iota((groups, rows), 0) == g_me, colst, 0.0), axis=0, keepdims=True)
    mine_col = jnp.sum(jnp.where(iota((rows, groups), 1) == g_me, cols, 0.0), axis=1, keepdims=True)
    by_source = dot(s_j, colst)
    term = (
        (by_source == (iota((rows, rows), 0) % width).astype(F32))
        & (mine_col == mine_row)
        & (mine_row >= 0)
    ).astype(F32)
    term = dot(j_s, term)
    source = iota((groups, rows), 0).astype(F32) * width + colst
    source = source.astype(I32)
    away = jnp.where((source // local) != (iota((groups, rows), 1) // local), term, 0.0)
    before = (iota((groups, groups), 1) < iota((groups, groups), 0)).astype(F32)
    count = jnp.sum(away, axis=0, keepdims=True)
    r0, r1 = iota((rows, rows), 0), iota((rows, rows), 1)
    earlier = ((r0 // local == r1 // local) & (r0 < r1)).astype(F32)
    rank = dot(before, away) + dot(jnp.broadcast_to(count, (8, rows)), earlier)[:1]
    rank = jnp.where(away > 0, rank, -1.0)
    slot = iota((slots, rows), 0).astype(F32)
    source_f = source.astype(F32)
    found = jnp.zeros((slots, rows), F32)
    for j in range(groups):
        found = found + jnp.where(rank[j : j + 1] == slot, source_f[j : j + 1], 0.0)
    fold = eq(iota((rows, row_devs), 0) // local, iota((rows, row_devs), 1))
    right_ref[...] = dot(found, fold).astype(I32)
    c0 = iota((cand, rows), 0)
    row_val = dot(eq(iota((cand, rows), 1), me * local + c0 // groups), cols)
    c1 = iota((cand, groups), 0)
    g1 = iota((cand, groups), 1)
    own = jnp.sum(jnp.where(g1 == c1 % groups, row_val, 0.0), axis=1, keepdims=True)
    q_1 = iota((cand, 1), 0) // groups
    j_1 = iota((cand, 1), 0) % groups
    s_1 = j_1 * width + own.astype(I32)
    s_val = dot(eq(iota((cand, rows), 1), s_1), cols)
    terms = ((own >= 0) & (row_val >= 0) & (s_val == row_val)).astype(F32)
    lefts = jnp.where(c1 % groups != g1, terms, 0.0)
    lower = (iota((cand, cand), 1) < iota((cand, cand), 0)).astype(F32)
    rank_l = dot(lower, lefts)
    marked = jnp.where(lefts > 0, rank_l, -1.0)
    piece = j_1 * local + q_1
    piece_f = piece.astype(F32)
    slot_g = iota((slots, groups), 0).astype(F32)
    got = jnp.zeros((slots, groups), F32)
    for k in range(cand):
        got = got + jnp.where(marked[k : k + 1] == slot_g, float((k % groups) * local + k // groups), 0.0)
    left_ref[...] = got.astype(I32)
    pick = g1 == g_me
    mine = jnp.sum(jnp.where(pick, terms, 0.0), axis=1, keepdims=True)
    l_rank = jnp.sum(jnp.where(pick, rank_l, 0.0), axis=1, keepdims=True)
    is_away = (s_1 // local != me).astype(F32)
    wide = iota((cand, 128), 1)
    both = jnp.where(wide == 0, mine, jnp.where(wide == 1, mine * is_away, 0.0))
    ranks = dot(lower, both)
    order = jnp.sum(jnp.where(wide == 0, ranks, 0.0), axis=1, keepdims=True)
    r_rank = jnp.sum(jnp.where(wide == 1, ranks, 0.0), axis=1, keepdims=True)
    l_at = jnp.where(j_1 == g_me, slots + q_1, l_rank.astype(I32))
    r_at = jnp.where(is_away > 0, r_rank.astype(I32), slots + s_1 % local)
    code = (q_1 + 4 * piece + 256 * l_at + 32768 * r_at).astype(F32)
    hot = (mine > 0) & (order == wide.astype(F32))
    code_ref[...] = jnp.sum(jnp.where(hot, code, 0.0), axis=0, keepdims=True).astype(I32)
    values = rows // groups
    copy = eq(iota((groups, rows), 1) % groups, iota((groups, rows), 0))
    has = eq(dot(cols, copy), (iota((rows, rows), 1) // groups).astype(F32))
    filled = eq(dot(cols, j_s), (r1 % width).astype(F32))
    far = jnp.where(r0 // local != r1 // local, filled, 0.0)
    group_of = eq(iota((row_devs, rows), 1) // local, iota((row_devs, rows), 0))
    back = eq(iota((rows, groups), 0) % groups, iota((rows, groups), 1))
    need_r = dot(dot(group_of, dot(far, has) * has), back)
    need_l = dot(dot(group_of, (dot(filled, has) - 1.0) * has), back)
    number = jnp.sum(mine, axis=(0, 1), keepdims=True)
    place = iota((1, 128), 1)
    info = jnp.where(place == 0, number, 0.0)
    for at, need in ((1, need_r), (2, need_l)):
        most = jnp.max(need, axis=(0, 1), keepdims=True)
        which = sum((most > size).astype(F32) for size in SIZES[:-1])
        info = info + jnp.where(place == at, which, 0.0)
    info_ref[...] = info.astype(I32)


def pack_kernel(size, table, pieces, out):
    def one(d, _):
        for slot in range(size):
            out[d, slot] = pieces[table[slot, d]]
        return 0

    lax.fori_loop(0, out.shape[0], one, 0)


def halves(block):
    high = block.astype(jnp.bfloat16)
    return high, (block - high.astype(F32)).astype(jnp.bfloat16)


def product(left, right):
    lh, ll = halves(left)
    rh, rl = halves(right)
    return dot(lh, rh) + (dot(lh, rl) + dot(ll, rh))


def unpack(size, came, blocks):
    tall = came.shape[2]

    def one(slot, _):
        for h in range(came.shape[0]):
            blocks[slot, h * tall : (h + 1) * tall, :] = came[h, slot]
        return 0

    lax.fori_loop(0, size, one, 0)


def unpack_kernel(size, came, blocks, buffer, sems):
    def out(slot):
        return pltpu.make_async_copy(buffer.at[slot], blocks.at[slot], sems.at[slot])

    unpack(size, came, buffer)

    def begin(slot, _):
        out(slot).start()
        return 0

    def end(slot, _):
        out(slot).wait()
        return 0

    lax.fori_loop(0, size, begin, 0)
    lax.fori_loop(0, size, end, 0)


def fetch_rights(code, many, x, rights, buffer, sems):
    local = x.shape[0]
    far = rights.shape[0]

    def begin(t, _):
        r_at = code[0, t] // 32768

        @pl.when(r_at < far)
        def _():
            pltpu.make_async_copy(rights.at[jnp.minimum(r_at, far - 1)], buffer.at[t], sems.at[t]).start()

        @pl.when(r_at >= far)
        def _():
            pltpu.make_async_copy(x.at[jnp.clip(r_at - far, 0, local - 1)], buffer.at[t], sems.at[t]).start()

        return 0

    lax.fori_loop(0, many, begin, 0)


def square_kernel(code, info, x, panel, rights, squared, spread, lefts, buffer, left_sems, right_sems):
    many = info[0, 0]

    def fetch(t):
        return pltpu.make_async_copy(panel.at[(code[0, t] // 4) % 64], lefts.at[t], left_sems.at[t])

    def begin(t, _):
        fetch(t).start()
        return 0

    lax.fori_loop(0, many, begin, 0)
    fetch_rights(code, many, x, rights, buffer, right_sems)
    squared[...] = jnp.zeros_like(squared)

    def one(t, _):
        fetch(t).wait()
        pltpu.make_async_copy(rights.at[0], buffer.at[t], right_sems.at[t]).wait()
        squared[code[0, t] % 4] += product(lefts[t], buffer[t])
        return 0

    lax.fori_loop(0, many, one, 0)
    tall = spread.shape[2]
    for k in range(spread.shape[0]):
        spread[k] = squared[:, k * tall : (k + 1) * tall, :]


def cube_kernel(size, code, info, x, squared, came, rights, purified, lefts, buffer, sems):
    local = x.shape[0]
    far = rights.shape[0]
    many = info[0, 0]
    fetch_rights(code, many, x, rights, buffer, sems)
    unpack(size, came, lefts)
    lefts[size : size + local] = squared[...]
    purified[...] = 3.0 * squared[...]

    def one(t, _):
        word = code[0, t]
        l_at = (word // 256) % 128
        pltpu.make_async_copy(rights.at[0], buffer.at[t], sems.at[t]).wait()
        left = lefts[jnp.where(l_at >= far, l_at - far + size, l_at)]
        purified[word % 4] += -2.0 * product(left, buffer[t])
        return 0

    lax.fori_loop(0, many, one, 0)


def shape(*dims, dtype=F32):
    return jax.ShapeDtypeStruct(dims, dtype)


def deliver(size, axis, table, held):
    _, tall, order = held.shape
    out = pl.pallas_call(
        functools.partial(pack_kernel, size),
        out_shape=shape(lax.axis_size(axis), size, tall, order),
        in_specs=[SMEM, VMEM],
        out_specs=VMEM,
        compiler_params=PARAMS,
        name="pack",
    )(table, held)
    return lax.all_to_all(out, axis, 0, 0, tiled=True)


def right_branch(size, table, held):
    came = deliver(size, "row", table, held)
    order = came.shape[3]
    return pl.pallas_call(
        functools.partial(unpack_kernel, size),
        out_shape=shape(table.shape[0], order, order),
        in_specs=[VMEM],
        out_specs=HBM,
        scratch_shapes=[pltpu.VMEM((size, order, order), F32), pltpu.SemaphoreType.DMA((size,))],
        compiler_params=PARAMS,
        name="unpack",
    )(came)


def left_branch(size, table, held, code, info, x, squared, rights):
    came = deliver(size, "col", table, held)
    local, order, _ = x.shape
    return pl.pallas_call(
        functools.partial(cube_kernel, size),
        out_shape=shape(local, order, order),
        in_specs=[SMEM, SMEM, VMEM, VMEM, VMEM, HBM],
        out_specs=VMEM,
        scratch_shapes=[
            pltpu.VMEM((size + local, order, order), F32),
            pltpu.VMEM((rights.shape[0], order, order), F32),
            pltpu.SemaphoreType.DMA((rights.shape[0],)),
        ],
        compiler_params=PARAMS,
        name="cube",
    )(code, info, x, squared, came, rights)


def body(density, columns):
    row_devs = lax.axis_size("row")
    rows, groups = columns.shape
    width = rows // groups
    local, _, order, _ = density.shape
    cand = local * groups
    fine, tall = order // row_devs, order // groups
    x = density[:, 0]
    panel = lax.all_gather(x, "col", axis=0, tiled=True)
    spread = x.reshape(local, row_devs, fine, order).transpose(1, 0, 2, 3)
    held = lax.all_to_all(spread, "row", 0, 0, tiled=True)
    held = held.reshape(row_devs * local, fine, order)
    here = jnp.stack([lax.axis_index("row"), lax.axis_index("col")]).astype(I32)
    cols = columns.astype(F32)
    right, left, code, info = pl.pallas_call(
        functools.partial(plan_kernel, rows, row_devs, groups, width),
        out_shape=(
            shape(cand, row_devs, dtype=I32),
            shape(cand, groups, dtype=I32),
            shape(1, 128, dtype=I32),
            shape(1, 128, dtype=I32),
        ),
        in_specs=[SMEM, VMEM, VMEM],
        out_specs=(VMEM, VMEM, VMEM, VMEM),
        compiler_params=PARAMS,
        name="plan",
    )(here, cols, cols.T)
    rights = lax.switch(
        info[0, 1], [functools.partial(right_branch, size) for size in SIZES], right, held
    )
    squared, spread = pl.pallas_call(
        square_kernel,
        out_shape=(shape(local, order, order), shape(groups, local, tall, order)),
        in_specs=[SMEM, SMEM, VMEM, HBM, HBM],
        out_specs=(VMEM, VMEM),
        scratch_shapes=[
            pltpu.VMEM((cand, order, order), F32),
            pltpu.VMEM((cand, order, order), F32),
            pltpu.SemaphoreType.DMA((cand,)),
            pltpu.SemaphoreType.DMA((cand,)),
        ],
        compiler_params=WIDE,
        name="square",
    )(code, info, x, panel, rights)
    held = lax.all_to_all(spread, "col", 0, 0, tiled=True)
    held = held.reshape(groups * local, tall, order)
    purified = lax.switch(
        info[0, 2],
        [functools.partial(left_branch, size) for size in SIZES],
        left,
        held,
        code,
        info,
        x,
        squared,
        rights,
    )
    return squared[:, None], purified[:, None]


def solution(mesh):
    return jax.shard_map(
        body,
        mesh=mesh,
        in_specs=(P("row", "col", None, None), P()),
        out_specs=(P("row", "col", None, None), P("row", "col", None, None)),
        check_vma=False,
    )
```

```python
import functools

import jax
import jax.numpy as jnp
from jax import lax
from jax.experimental import pallas as pl
from jax.experimental.pallas import tpu as pltpu
from jax.sharding import PartitionSpec as P

F32 = jnp.float32
I32 = jnp.int32
VMEM = pl.BlockSpec(memory_space=pltpu.VMEM)
HBM = pl.BlockSpec(memory_space=pltpu.HBM)
SMEM = pl.BlockSpec(memory_space=pltpu.SMEM)
PARAMS = pltpu.CompilerParams(vmem_limit_bytes=24 << 20)
SIZES = (6, 7, 8, 9, 10, 11, 12, 13, 14, 16, 20)
EVERY = 64
STEP = 2


def iota(shape, dim):
    return lax.broadcasted_iota(I32, shape, dim)


def eq(a, b):
    return (a == b).astype(F32)


def dot(a, b):
    return jnp.dot(a, b, preferred_element_type=F32)


def plan_kernel(rows, row_devs, groups, width, here, cols_ref, colst_ref, right_ref, left_ref, code_ref, info_ref):
    me, g_me = here[0], here[1]
    local = rows // row_devs
    cand = local * groups
    slots = cand
    cols = cols_ref[...]
    colst = colst_ref[...]
    s_j = eq(iota((rows, groups), 0) // width, iota((rows, groups), 1))
    j_s = eq(iota((groups, rows), 1) // width, iota((groups, rows), 0))
    mine_row = jnp.sum(jnp.where(iota((groups, rows), 0) == g_me, colst, 0.0), axis=0, keepdims=True)
    mine_col = jnp.sum(jnp.where(iota((rows, groups), 1) == g_me, cols, 0.0), axis=1, keepdims=True)
    by_source = dot(s_j, colst)
    term = (
        (by_source == (iota((rows, rows), 0) % width).astype(F32))
        & (mine_col == mine_row)
        & (mine_row >= 0)
    ).astype(F32)
    term = dot(j_s, term)
    source = iota((groups, rows), 0).astype(F32) * width + colst
    source = source.astype(I32)
    away = jnp.where((source // local) != (iota((groups, rows), 1) // local), term, 0.0)
    before = (iota((groups, groups), 1) < iota((groups, groups), 0)).astype(F32)
    count = jnp.sum(away, axis=0, keepdims=True)
    r0, r1 = iota((rows, rows), 0), iota((rows, rows), 1)
    earlier = ((r0 // local == r1 // local) & (r0 < r1)).astype(F32)
    rank = dot(before, away) + dot(jnp.broadcast_to(count, (8, rows)), earlier)[:1]
    rank = jnp.where(away > 0, rank, -1.0)
    slot = iota((slots, rows), 0).astype(F32)
    source_f = source.astype(F32)
    found = jnp.zeros((slots, rows), F32)
    for j in range(groups):
        found = found + jnp.where(rank[j : j + 1] == slot, source_f[j : j + 1], 0.0)
    fold = eq(iota((rows, row_devs), 0) // local, iota((rows, row_devs), 1))
    right_ref[...] = dot(found, fold).astype(I32)
    c0 = iota((cand, rows), 0)
    row_val = dot(eq(iota((cand, rows), 1), me * local + c0 // groups), cols)
    c1 = iota((cand, groups), 0)
    g1 = iota((cand, groups), 1)
    own = jnp.sum(jnp.where(g1 == c1 % groups, row_val, 0.0), axis=1, keepdims=True)
    q_1 = iota((cand, 1), 0) // groups
    j_1 = iota((cand, 1), 0) % groups
    s_1 = j_1 * width + own.astype(I32)
    s_val = dot(eq(iota((cand, rows), 1), s_1), cols)
    terms = ((own >= 0) & (row_val >= 0) & (s_val == row_val)).astype(F32)
    lefts = jnp.where(c1 % groups != g1, terms, 0.0)
    lower = (iota((cand, cand), 1) < iota((cand, cand), 0)).astype(F32)
    rank_l = dot(lower, lefts)
    marked = jnp.where(lefts > 0, rank_l, -1.0)
    piece = j_1 * local + q_1
    piece_f = piece.astype(F32)
    slot_g = iota((slots, groups), 0).astype(F32)
    got = jnp.zeros((slots, groups), F32)
    for k in range(cand):
        got = got + jnp.where(marked[k : k + 1] == slot_g, float((k % groups) * local + k // groups), 0.0)
    left_ref[...] = got.astype(I32)
    pick = g1 == g_me
    mine = jnp.sum(jnp.where(pick, terms, 0.0), axis=1, keepdims=True)
    l_rank = jnp.sum(jnp.where(pick, rank_l, 0.0), axis=1, keepdims=True)
    is_away = (s_1 // local != me).astype(F32)
    wide = iota((cand, 128), 1)
    both = jnp.where(wide == 0, mine, jnp.where(wide == 1, mine * is_away, 0.0))
    ranks = dot(lower, both)
    order = jnp.sum(jnp.where(wide == 0, ranks, 0.0), axis=1, keepdims=True)
    r_rank = jnp.sum(jnp.where(wide == 1, ranks, 0.0), axis=1, keepdims=True)
    l_at = jnp.where(j_1 == g_me, slots + q_1, l_rank.astype(I32))
    r_at = jnp.where(is_away > 0, r_rank.astype(I32), slots + s_1 % local)
    half = (j_1 // 2) % 2 != (g_me // 2) % 2
    panel_at = ((j_1 // 4) * 2 + j_1 % 2) * 2 + half.astype(I32)
    panel_at = panel_at * local + q_1
    code = (q_1 + 8 * panel_at + 512 * l_at + 65536 * r_at).astype(F32)
    idle = float(local + 512 * slots + 65536 * slots)
    hot = (mine > 0) & (order == wide.astype(F32))
    code = jnp.sum(jnp.where(hot, code - idle, 0.0), axis=0, keepdims=True) + idle
    code_ref[...] = code.astype(I32)
    values = rows // groups
    copy = eq(iota((groups, rows), 1) % groups, iota((groups, rows), 0))
    has = eq(dot(cols, copy), (iota((rows, rows), 1) // groups).astype(F32))
    filled = eq(dot(cols, j_s), (r1 % width).astype(F32))
    far = jnp.where(r0 // local != r1 // local, filled, 0.0)
    group_of = eq(iota((row_devs, rows), 1) // local, iota((row_devs, rows), 0))
    back = eq(iota((rows, groups), 0) % groups, iota((rows, groups), 1))
    need_r = dot(dot(group_of, dot(far, has) * has), back)
    need_l = dot(dot(group_of, (dot(filled, has) - 1.0) * has), back)
    number = jnp.sum(mine, axis=(0, 1), keepdims=True)
    place = iota((1, 128), 1)
    which_r, which_l = (
        sum((jnp.max(need, axis=(0, 1), keepdims=True) > size).astype(F32) for size in SIZES)
        for need in (need_r, need_l)
    )
    which_l = jnp.where(which_r == len(SIZES), which_r, which_l)
    info = jnp.where(place == 0, number, jnp.where(place == 1, which_r, which_l))
    info_ref[...] = info.astype(I32)


def pack_kernel(size, table, pieces, out):
    def one(d, _):
        for slot in range(size):
            out[d, slot] = pieces[table[slot, d]]
        return 0

    lax.fori_loop(0, out.shape[0], one, 0)


def halves(block, axis):
    high = block.astype(jnp.bfloat16)
    low = (block - high.astype(F32)).astype(jnp.bfloat16)
    return jnp.concatenate([high, low], axis=axis)


def product(left, right):
    n = left.shape[0]
    full = dot(halves(left, 0), halves(right, 1))
    return full[:n, :n] + (full[:n, n:] + full[n:, :n])


def unpack(size, came, blocks):
    tall = came.shape[2]

    def one(slot, _):
        for h in range(came.shape[0]):
            blocks[slot, h * tall : (h + 1) * tall, :] = came[h, slot]
        return 0

    lax.fori_loop(0, size, one, 0)


def unpack_kernel(size, came, x, blocks):
    unpack(size, came, blocks)
    blocks[blocks.shape[0] - x.shape[0] :] = x[...]


def place(at, room):
    return jnp.where(at >= EVERY, at - EVERY + room, jnp.minimum(at, room - 1))


def add_terms(code, steps, total, blocks_of):
    def one(step, _):
        words = [code[0, step * STEP + k] for k in range(STEP)]
        terms = [product(*blocks_of(step * STEP + k, words[k])) for k in range(STEP)]
        for word, term in zip(words, terms):
            total[word % 8] += term
        return 0

    lax.fori_loop(0, steps, one, 0)


def square_kernel(code, info, panel, rights, squared, spread, lefts, total, sems):
    local = squared.shape[0]
    steps = (info[0, 0] + STEP - 1) // STEP
    room = rights.shape[0] - local

    def fetch(t):
        return pltpu.make_async_copy(panel.at[(code[0, t] // 8) % 64], lefts.at[t], sems.at[t])

    def begin(t, _):
        fetch(t).start()
        return 0

    lax.fori_loop(0, steps * STEP, begin, 0)
    total[...] = jnp.zeros_like(total)

    def blocks_of(t, word):
        fetch(t).wait()
        return lefts[t], rights[place(word // 65536, room)]

    add_terms(code, steps, total, blocks_of)
    squared[...] = total[:local]
    tall = spread.shape[2]
    for k in range(spread.shape[0]):
        spread[k] = squared[:, k * tall : (k + 1) * tall, :]


def cube_kernel(size, code, info, squared, came, rights, purified, lefts, total):
    local = squared.shape[0]
    room = rights.shape[0] - local
    unpack(size, came, lefts)
    lefts[size : size + local] = squared[...]
    total[...] = jnp.zeros_like(total)

    def blocks_of(t, word):
        return lefts[place((word // 512) % 128, size)], rights[place(word // 65536, room)]

    add_terms(code, (info[0, 0] + STEP - 1) // STEP, total, blocks_of)
    purified[...] = 3.0 * squared[...] - 2.0 * total[:local]


def shape(*dims, dtype=F32):
    return jax.ShapeDtypeStruct(dims, dtype)


def deliver(size, axis, table, held):
    _, tall, order = held.shape
    out = pl.pallas_call(
        functools.partial(pack_kernel, size),
        out_shape=shape(lax.axis_size(axis), size, tall, order),
        in_specs=[SMEM, VMEM],
        out_specs=VMEM,
        compiler_params=PARAMS,
        name="pack",
    )(table, held)
    return lax.all_to_all(out, axis, 0, 0, tiled=True)


def get_rights(size, room, table, held, x):
    came = deliver(size, "row", table, held)
    local, order, _ = x.shape
    return pl.pallas_call(
        functools.partial(unpack_kernel, size),
        out_shape=shape(room + local, order, order),
        in_specs=[VMEM, VMEM],
        out_specs=VMEM,
        compiler_params=PARAMS,
        name="unpack",
    )(came, x)


def no_rights(room, table, held, x):
    return jnp.zeros((room + x.shape[0], *x.shape[1:]), F32)


def finish(size, tables, held, code, info, x, panel, rights):
    right, left = tables
    local, order, _ = x.shape
    groups = lax.axis_size("col")
    tall = order // groups
    if size == EVERY:
        rights = get_rights(EVERY, EVERY, right, held, x)
    squared, spread = pl.pallas_call(
        square_kernel,
        out_shape=(shape(local, order, order), shape(groups, local, tall, order)),
        in_specs=[SMEM, SMEM, HBM, VMEM],
        out_specs=(VMEM, VMEM),
        scratch_shapes=[
            pltpu.VMEM((EVERY, order, order), F32),
            pltpu.VMEM((local + 1, order, order), F32),
            pltpu.SemaphoreType.DMA((EVERY,)),
        ],
        compiler_params=PARAMS,
        name="square",
    )(code, info, panel, rights)
    held = lax.all_to_all(spread, "col", 0, 0, tiled=True)
    came = deliver(size, "col", left, held.reshape(groups * local, tall, order))
    purified = pl.pallas_call(
        functools.partial(cube_kernel, size),
        out_shape=shape(local, order, order),
        in_specs=[SMEM, SMEM, VMEM, VMEM, VMEM],
        out_specs=VMEM,
        scratch_shapes=[
            pltpu.VMEM((size + local, order, order), F32),
            pltpu.VMEM((local + 1, order, order), F32),
        ],
        compiler_params=PARAMS,
        name="cube",
    )(code, info, squared, came, rights)
    return squared, purified


def body(density, columns):
    row_devs = lax.axis_size("row")
    rows, groups = columns.shape
    width = rows // groups
    local, _, order, _ = density.shape
    cand = local * groups
    fine, tall = order // row_devs, order // groups
    x = density[:, 0]
    spread = x.reshape(local, row_devs, fine, order).transpose(1, 0, 2, 3)
    held = lax.all_to_all(spread, "row", 0, 0, tiled=True)
    held = held.reshape(row_devs * local, fine, order)
    here = jnp.stack([lax.axis_index("row"), lax.axis_index("col")]).astype(I32)
    cols = columns.astype(F32)
    right, left, code, info = pl.pallas_call(
        functools.partial(plan_kernel, rows, row_devs, groups, width),
        out_shape=(
            shape(cand, row_devs, dtype=I32),
            shape(cand, groups, dtype=I32),
            shape(1, 128, dtype=I32),
            shape(1, 128, dtype=I32),
        ),
        in_specs=[SMEM, VMEM, VMEM],
        out_specs=(VMEM, VMEM, VMEM, VMEM),
        compiler_params=PARAMS,
        name="plan",
    )(here, cols, cols.T)
    mate = lax.ppermute(x, "col", [(k, k ^ 2) for k in range(groups)])
    alike = [[k for k in range(groups) if (k // 2) % 2 == half] for half in range(2)]
    mate, held, _ = lax.optimization_barrier((mate, held, info))
    panel = lax.all_gather(
        jnp.concatenate([x, mate]), "col", axis=0, tiled=True, axis_index_groups=alike
    )
    room = SIZES[-1]
    rights = lax.switch(
        info[0, 1],
        [functools.partial(get_rights, size, room) for size in SIZES] + [functools.partial(no_rights, room)],
        right,
        held,
        x,
    )
    squared, purified = lax.switch(
        info[0, 2],
        [functools.partial(finish, size) for size in (*SIZES, EVERY)],
        (right, left),
        held,
        code,
        info,
        x,
        panel,
        rights,
    )
    return squared[:, None], purified[:, None]


def solution(mesh):
    return jax.shard_map(
        body,
        mesh=mesh,
        in_specs=(P("row", "col", None, None), P()),
        out_specs=(P("row", "col", None, None), P("row", "col", None, None)),
        check_vma=False,
    )
```

```python
import functools

import jax
import jax.numpy as jnp
from jax import lax
from jax.experimental import pallas as pl
from jax.experimental.pallas import tpu as pltpu
from jax.sharding import PartitionSpec as P

F32 = jnp.float32
I32 = jnp.int32
VMEM = pl.BlockSpec(memory_space=pltpu.VMEM)
HBM = pl.BlockSpec(memory_space=pltpu.HBM)
SMEM = pl.BlockSpec(memory_space=pltpu.SMEM)
PARAMS = pltpu.CompilerParams(vmem_limit_bytes=24 << 20)
SIZES = (6, 7, 8, 9, 10, 11, 12, 13, 14, 16, 20, 64)
EVERY = SIZES[-1]
STEP = 2


def iota(shape, dim):
    return lax.broadcasted_iota(I32, shape, dim)


def eq(a, b):
    return (a == b).astype(F32)


def dot(a, b):
    return jnp.dot(a, b, preferred_element_type=F32)


def plan_kernel(rows, row_devs, groups, width, here, cols_ref, colst_ref, right_ref, left_ref, code_ref, info_ref):
    me, g_me = here[0], here[1]
    local = rows // row_devs
    cand = local * groups
    slots = cand
    cols = cols_ref[...]
    colst = colst_ref[...]
    s_j = eq(iota((rows, groups), 0) // width, iota((rows, groups), 1))
    j_s = eq(iota((groups, rows), 1) // width, iota((groups, rows), 0))
    mine_row = jnp.sum(jnp.where(iota((groups, rows), 0) == g_me, colst, 0.0), axis=0, keepdims=True)
    mine_col = jnp.sum(jnp.where(iota((rows, groups), 1) == g_me, cols, 0.0), axis=1, keepdims=True)
    by_source = dot(s_j, colst)
    term = (
        (by_source == (iota((rows, rows), 0) % width).astype(F32))
        & (mine_col == mine_row)
        & (mine_row >= 0)
    ).astype(F32)
    term = dot(j_s, term)
    source = iota((groups, rows), 0).astype(F32) * width + colst
    source = source.astype(I32)
    away = jnp.where((source // local) != (iota((groups, rows), 1) // local), term, 0.0)
    before = (iota((groups, groups), 1) < iota((groups, groups), 0)).astype(F32)
    count = jnp.sum(away, axis=0, keepdims=True)
    r0, r1 = iota((rows, rows), 0), iota((rows, rows), 1)
    earlier = ((r0 // local == r1 // local) & (r0 < r1)).astype(F32)
    rank = dot(before, away) + dot(jnp.broadcast_to(count, (8, rows)), earlier)[:1]
    rank = jnp.where(away > 0, rank, -1.0)
    slot = iota((slots, rows), 0).astype(F32)
    source_f = source.astype(F32)
    found = jnp.zeros((slots, rows), F32)
    for j in range(groups):
        found = found + jnp.where(rank[j : j + 1] == slot, source_f[j : j + 1], 0.0)
    fold = eq(iota((rows, row_devs), 0) // local, iota((rows, row_devs), 1))
    right_ref[...] = dot(found, fold).astype(I32)
    c0 = iota((cand, rows), 0)
    row_val = dot(eq(iota((cand, rows), 1), me * local + c0 // groups), cols)
    c1 = iota((cand, groups), 0)
    g1 = iota((cand, groups), 1)
    own = jnp.sum(jnp.where(g1 == c1 % groups, row_val, 0.0), axis=1, keepdims=True)
    q_1 = iota((cand, 1), 0) // groups
    j_1 = iota((cand, 1), 0) % groups
    s_1 = j_1 * width + own.astype(I32)
    s_val = dot(eq(iota((cand, rows), 1), s_1), cols)
    terms = ((own >= 0) & (row_val >= 0) & (s_val == row_val)).astype(F32)
    lefts = jnp.where(c1 % groups != g1, terms, 0.0)
    lower = (iota((cand, cand), 1) < iota((cand, cand), 0)).astype(F32)
    rank_l = dot(lower, lefts)
    marked = jnp.where(lefts > 0, rank_l, -1.0)
    piece = j_1 * local + q_1
    piece_f = piece.astype(F32)
    slot_g = iota((slots, groups), 0).astype(F32)
    got = jnp.zeros((slots, groups), F32)
    for k in range(cand):
        got = got + jnp.where(marked[k : k + 1] == slot_g, float((k % groups) * local + k // groups), 0.0)
    left_ref[...] = got.astype(I32)
    pick = g1 == g_me
    mine = jnp.sum(jnp.where(pick, terms, 0.0), axis=1, keepdims=True)
    l_rank = jnp.sum(jnp.where(pick, rank_l, 0.0), axis=1, keepdims=True)
    is_away = (s_1 // local != me).astype(F32)
    wide = iota((cand, 128), 1)
    both = jnp.where(wide == 0, mine, jnp.where(wide == 1, mine * is_away, 0.0))
    ranks = dot(lower, both)
    order = jnp.sum(jnp.where(wide == 0, ranks, 0.0), axis=1, keepdims=True)
    r_rank = jnp.sum(jnp.where(wide == 1, ranks, 0.0), axis=1, keepdims=True)
    l_at = jnp.where(j_1 == g_me, slots + q_1, l_rank.astype(I32))
    r_at = jnp.where(is_away > 0, r_rank.astype(I32), slots + s_1 % local)
    half = (j_1 // 2) % 2 != (g_me // 2) % 2
    panel_at = ((j_1 // 4) * 2 + j_1 % 2) * 2 + half.astype(I32)
    panel_at = panel_at * local + q_1
    code = (q_1 + 8 * panel_at + 512 * l_at + 65536 * r_at).astype(F32)
    idle = float(local + 512 * slots + 65536 * slots)
    hot = (mine > 0) & (order == wide.astype(F32))
    code = jnp.sum(jnp.where(hot, code - idle, 0.0), axis=0, keepdims=True) + idle
    code_ref[...] = code.astype(I32)
    values = rows // groups
    copy = eq(iota((groups, rows), 1) % groups, iota((groups, rows), 0))
    has = eq(dot(cols, copy), (iota((rows, rows), 1) // groups).astype(F32))
    filled = eq(dot(cols, j_s), (r1 % width).astype(F32))
    far = jnp.where(r0 // local != r1 // local, filled, 0.0)
    group_of = eq(iota((row_devs, rows), 1) // local, iota((row_devs, rows), 0))
    back = eq(iota((rows, groups), 0) % groups, iota((rows, groups), 1))
    need_r = dot(dot(group_of, dot(far, has) * has), back)
    need_l = dot(dot(group_of, (dot(filled, has) - 1.0) * has), back)
    number = jnp.sum(mine, axis=(0, 1), keepdims=True)
    most = jnp.max(jnp.maximum(need_r, need_l), axis=(0, 1), keepdims=True)
    which = sum((most > size).astype(F32) for size in SIZES[:-1])
    info_ref[...] = jnp.where(iota((1, 128), 1) == 0, number, which).astype(I32)


def pack_kernel(size, table, pieces, out):
    def one(d, _):
        for slot in range(size):
            out[d, slot] = pieces[table[slot, d]]
        return 0

    lax.fori_loop(0, out.shape[0], one, 0)


def halves(block, axis):
    high = block.astype(jnp.bfloat16)
    low = (block - high.astype(F32)).astype(jnp.bfloat16)
    return jnp.concatenate([high, low], axis=axis)


def product(left, right):
    n = left.shape[0]
    full = dot(halves(left, 0), halves(right, 1))
    return full[:n, :n] + (full[:n, n:] + full[n:, :n])


def unpack(size, came, blocks):
    tall = came.shape[2]

    def one(slot, _):
        for h in range(came.shape[0]):
            blocks[slot, h * tall : (h + 1) * tall, :] = came[h, slot]
        return 0

    lax.fori_loop(0, size, one, 0)


def place(at, room):
    return jnp.where(at >= EVERY, at - EVERY + room, jnp.minimum(at, room - 1))


def add_terms(code, steps, total, blocks_of):
    def one(step, _):
        words = [code[0, step * STEP + k] for k in range(STEP)]
        terms = [product(*blocks_of(step * STEP + k, words[k])) for k in range(STEP)]
        for word, term in zip(words, terms):
            total[word % 8] += term
        return 0

    lax.fori_loop(0, steps, one, 0)


def fetch_kernel(code, info, panel, lefts, sems):
    many = (info[0, 0] + STEP - 1) // STEP * STEP

    def copy(t):
        return pltpu.make_async_copy(panel.at[(code[0, t] // 8) % 64], lefts.at[t], sems.at[t])

    def begin(t, _):
        copy(t).start()
        return 0

    def end(t, _):
        copy(t).wait()
        return 0

    lax.fori_loop(0, many, begin, 0)
    lax.fori_loop(0, many, end, 0)


def square_kernel(size, code, info, x, lefts, came, squared, spread, rights, total):
    local = x.shape[0]
    unpack(size, came, rights)
    rights[size:] = x[...]
    total[...] = jnp.zeros_like(total)

    def blocks_of(t, word):
        return lefts[t], rights[place(word // 65536, size)]

    add_terms(code, (info[0, 0] + STEP - 1) // STEP, total, blocks_of)
    squared[...] = total[:local]
    tall = spread.shape[2]
    for k in range(spread.shape[0]):
        spread[k] = squared[:, k * tall : (k + 1) * tall, :]


def cube_kernel(size, code, info, squared, came, rights, purified, lefts, total):
    local = squared.shape[0]
    unpack(size, came, lefts)
    lefts[size : size + local] = squared[...]
    total[...] = jnp.zeros_like(total)

    def blocks_of(t, word):
        return lefts[place((word // 512) % 128, size)], rights[place(word // 65536, size)]

    add_terms(code, (info[0, 0] + STEP - 1) // STEP, total, blocks_of)
    purified[...] = 3.0 * squared[...] - 2.0 * total[:local]


def shape(*dims, dtype=F32):
    return jax.ShapeDtypeStruct(dims, dtype)


def deliver(size, axis, table, held):
    _, tall, order = held.shape
    out = pl.pallas_call(
        functools.partial(pack_kernel, size),
        out_shape=shape(lax.axis_size(axis), size, tall, order),
        in_specs=[SMEM, VMEM],
        out_specs=VMEM,
        compiler_params=PARAMS,
        name="pack",
    )(table, held)
    return lax.all_to_all(out, axis, 0, 0, tiled=True)


def branch(size, tables, code, info, x, both, held, alike):
    right, left = tables
    local, order, _ = x.shape
    groups = lax.axis_size("col")
    tall = order // groups
    panel = lax.all_gather(both, "col", axis=0, tiled=True, axis_index_groups=alike)
    came = deliver(size, "row", right, held)
    lefts = pl.pallas_call(
        fetch_kernel,
        out_shape=shape(size + local + 1, order, order),
        in_specs=[SMEM, SMEM, HBM],
        out_specs=VMEM,
        scratch_shapes=[pltpu.SemaphoreType.DMA((size + local + 1,))],
        compiler_params=PARAMS,
        name="fetch",
    )(code, info, panel)
    squared, spread, rights = pl.pallas_call(
        functools.partial(square_kernel, size),
        out_shape=(
            shape(local, order, order),
            shape(groups, local, tall, order),
            shape(size + local, order, order),
        ),
        in_specs=[SMEM, SMEM, VMEM, VMEM, VMEM],
        out_specs=(VMEM, VMEM, VMEM),
        scratch_shapes=[pltpu.VMEM((local + 1, order, order), F32)],
        compiler_params=PARAMS,
        name="square",
    )(code, info, x, lefts, came)
    held = lax.all_to_all(spread, "col", 0, 0, tiled=True)
    came = deliver(size, "col", left, held.reshape(groups * local, tall, order))
    purified = pl.pallas_call(
        functools.partial(cube_kernel, size),
        out_shape=shape(local, order, order),
        in_specs=[SMEM, SMEM, VMEM, VMEM, VMEM],
        out_specs=VMEM,
        scratch_shapes=[
            pltpu.VMEM((size + local, order, order), F32),
            pltpu.VMEM((local + 1, order, order), F32),
        ],
        compiler_params=PARAMS,
        name="cube",
    )(code, info, squared, came, rights)
    return squared, purified


def body(density, columns):
    row_devs = lax.axis_size("row")
    rows, groups = columns.shape
    width = rows // groups
    local, _, order, _ = density.shape
    cand = local * groups
    fine, tall = order // row_devs, order // groups
    x = density[:, 0]
    spread = x.reshape(local, row_devs, fine, order).transpose(1, 0, 2, 3)
    held = lax.all_to_all(spread, "row", 0, 0, tiled=True)
    held = held.reshape(row_devs * local, fine, order)
    here = jnp.stack([lax.axis_index("row"), lax.axis_index("col")]).astype(I32)
    cols = columns.astype(F32)
    right, left, code, info = pl.pallas_call(
        functools.partial(plan_kernel, rows, row_devs, groups, width),
        out_shape=(
            shape(cand, row_devs, dtype=I32),
            shape(cand, groups, dtype=I32),
            shape(1, 128, dtype=I32),
            shape(1, 128, dtype=I32),
        ),
        in_specs=[SMEM, VMEM, VMEM],
        out_specs=(VMEM, VMEM, VMEM, VMEM),
        compiler_params=PARAMS,
        name="plan",
    )(here, cols, cols.T)
    mate = lax.ppermute(x, "col", [(k, k ^ 2) for k in range(groups)])
    alike = [[k for k in range(groups) if (k // 2) % 2 == half] for half in range(2)]
    both = jnp.concatenate([x, mate])
    which, both, held = lax.optimization_barrier((info[0, 1], both, held))
    squared, purified = lax.switch(
        which,
        [functools.partial(branch, size, alike=alike) for size in SIZES],
        (right, left),
        code,
        info,
        x,
        both,
        held,
    )
    return squared[:, None], purified[:, None]


def solution(mesh):
    return jax.shard_map(
        body,
        mesh=mesh,
        in_specs=(P("row", "col", None, None), P()),
        out_specs=(P("row", "col", None, None), P("row", "col", None, None)),
        check_vma=False,
    )
```

```python
import functools

import jax
import jax.numpy as jnp
from jax import lax
from jax.experimental import pallas as pl
from jax.experimental.pallas import tpu as pltpu
from jax.sharding import PartitionSpec as P

F32 = jnp.float32
I32 = jnp.int32
VMEM = pl.BlockSpec(memory_space=pltpu.VMEM)
HBM = pl.BlockSpec(memory_space=pltpu.HBM)
SMEM = pl.BlockSpec(memory_space=pltpu.SMEM)
PARAMS = pltpu.CompilerParams(vmem_limit_bytes=24 << 20)
SIZES = (6, 7, 8, 9, 10, 11, 12, 13, 14, 16, 20, 64)
EVERY = SIZES[-1]
STEP = 2


def iota(shape, dim):
    return lax.broadcasted_iota(I32, shape, dim)


def eq(a, b):
    return (a == b).astype(F32)


def dot(a, b):
    return jnp.dot(a, b, preferred_element_type=F32)


def plan_kernel(rows, row_devs, groups, width, here, cols_ref, colst_ref, right_ref, left_ref, code_ref, info_ref):
    me, g_me = here[0], here[1]
    local = rows // row_devs
    cand = local * groups
    slots = cand
    cols = cols_ref[...]
    colst = colst_ref[...]
    s_j = eq(iota((rows, groups), 0) // width, iota((rows, groups), 1))
    j_s = eq(iota((groups, rows), 1) // width, iota((groups, rows), 0))
    mine_row = jnp.sum(jnp.where(iota((groups, rows), 0) == g_me, colst, 0.0), axis=0, keepdims=True)
    mine_col = jnp.sum(jnp.where(iota((rows, groups), 1) == g_me, cols, 0.0), axis=1, keepdims=True)
    by_source = dot(s_j, colst)
    term = (
        (by_source == (iota((rows, rows), 0) % width).astype(F32))
        & (mine_col == mine_row)
        & (mine_row >= 0)
    ).astype(F32)
    term = dot(j_s, term)
    source = iota((groups, rows), 0).astype(F32) * width + colst
    source = source.astype(I32)
    away = jnp.where((source // local) != (iota((groups, rows), 1) // local), term, 0.0)
    before = (iota((groups, groups), 1) < iota((groups, groups), 0)).astype(F32)
    count = jnp.sum(away, axis=0, keepdims=True)
    r0, r1 = iota((rows, rows), 0), iota((rows, rows), 1)
    earlier = ((r0 // local == r1 // local) & (r0 < r1)).astype(F32)
    rank = dot(before, away) + dot(jnp.broadcast_to(count, (8, rows)), earlier)[:1]
    rank = jnp.where(away > 0, rank, -1.0)
    slot = iota((slots, rows), 0).astype(F32)
    source_f = source.astype(F32)
    found = jnp.zeros((slots, rows), F32)
    for j in range(groups):
        found = found + jnp.where(rank[j : j + 1] == slot, source_f[j : j + 1], 0.0)
    fold = eq(iota((rows, row_devs), 0) // local, iota((rows, row_devs), 1))
    right_ref[...] = dot(found, fold).astype(I32)
    c0 = iota((cand, rows), 0)
    row_val = dot(eq(iota((cand, rows), 1), me * local + c0 // groups), cols)
    c1 = iota((cand, groups), 0)
    g1 = iota((cand, groups), 1)
    own = jnp.sum(jnp.where(g1 == c1 % groups, row_val, 0.0), axis=1, keepdims=True)
    q_1 = iota((cand, 1), 0) // groups
    j_1 = iota((cand, 1), 0) % groups
    s_1 = j_1 * width + own.astype(I32)
    s_val = dot(eq(iota((cand, rows), 1), s_1), cols)
    terms = ((own >= 0) & (row_val >= 0) & (s_val == row_val)).astype(F32)
    lefts = jnp.where(c1 % groups != g1, terms, 0.0)
    lower = (iota((cand, cand), 1) < iota((cand, cand), 0)).astype(F32)
    rank_l = dot(lower, lefts)
    marked = jnp.where(lefts > 0, rank_l, -1.0)
    piece = j_1 * local + q_1
    piece_f = piece.astype(F32)
    slot_g = iota((slots, groups), 0).astype(F32)
    got = jnp.zeros((slots, groups), F32)
    for k in range(cand):
        got = got + jnp.where(marked[k : k + 1] == slot_g, float((k % groups) * local + k // groups), 0.0)
    left_ref[...] = got.astype(I32)
    pick = g1 == g_me
    mine = jnp.sum(jnp.where(pick, terms, 0.0), axis=1, keepdims=True)
    l_rank = jnp.sum(jnp.where(pick, rank_l, 0.0), axis=1, keepdims=True)
    is_away = (s_1 // local != me).astype(F32)
    wide = iota((cand, 128), 1)
    both = jnp.where(wide == 0, mine, jnp.where(wide == 1, mine * is_away, 0.0))
    ranks = dot(lower, both)
    order = jnp.sum(jnp.where(wide == 0, ranks, 0.0), axis=1, keepdims=True)
    r_rank = jnp.sum(jnp.where(wide == 1, ranks, 0.0), axis=1, keepdims=True)
    l_at = jnp.where(j_1 == g_me, slots + q_1, l_rank.astype(I32))
    r_at = jnp.where(is_away > 0, r_rank.astype(I32), slots + s_1 % local)
    half = (j_1 // 2) % 2 != (g_me // 2) % 2
    panel_at = ((j_1 // 4) * 2 + j_1 % 2) * 2 + half.astype(I32)
    panel_at = panel_at * local + q_1
    code = (q_1 + 8 * panel_at + 512 * l_at + 65536 * r_at).astype(F32)
    idle = float(local + 512 * slots + 65536 * slots)
    hot = (mine > 0) & (order == wide.astype(F32))
    code = jnp.sum(jnp.where(hot, code - idle, 0.0), axis=0, keepdims=True) + idle
    code_ref[...] = code.astype(I32)
    values = rows // groups
    copy = eq(iota((groups, rows), 1) % groups, iota((groups, rows), 0))
    has = eq(dot(cols, copy), (iota((rows, rows), 1) // groups).astype(F32))
    filled = eq(dot(cols, j_s), (r1 % width).astype(F32))
    far = jnp.where(r0 // local != r1 // local, filled, 0.0)
    group_of = eq(iota((row_devs, rows), 1) // local, iota((row_devs, rows), 0))
    back = eq(iota((rows, groups), 0) % groups, iota((rows, groups), 1))
    need_r = dot(dot(group_of, dot(far, has) * has), back)
    need_l = dot(dot(group_of, (dot(filled, has) - 1.0) * has), back)
    number = jnp.sum(mine, axis=(0, 1), keepdims=True)
    most = jnp.max(jnp.maximum(need_r, need_l), axis=(0, 1), keepdims=True)
    which = sum((most > size).astype(F32) for size in SIZES[:-1])
    info_ref[...] = jnp.where(iota((1, 128), 1) == 0, number, which).astype(I32)


def pack_kernel(size, table, pieces, out):
    def one(step, _):
        for d in [step * 4 + k for k in range(4)]:
            for slot in range(size):
                out[d, slot] = pieces[table[slot, d]]
        return 0

    lax.fori_loop(0, out.shape[0] // 4, one, 0)


def spread_kernel(x, out, sems):
    copies = [pltpu.make_async_copy(x.at[b], out.at[:, b], sems.at[b]) for b in range(x.shape[0])]
    for copy in copies:
        copy.start()
    for copy in copies:
        copy.wait()


def halves(block):
    high = block.astype(jnp.bfloat16)
    return high, (block - high.astype(F32)).astype(jnp.bfloat16)


def product(left, right):
    lh, ll = halves(left)
    rh, rl = halves(right)
    return dot(jnp.concatenate([lh, lh, ll], axis=1), jnp.concatenate([rh, rl, rh], axis=0))


def unpack(size, came, blocks):
    tall = came.shape[2]

    def one(slot, _):
        for h in range(came.shape[0]):
            blocks[slot, h * tall : (h + 1) * tall, :] = came[h, slot]
        return 0

    lax.fori_loop(0, size, one, 0)


def place(at, room):
    return jnp.where(at >= EVERY, at - EVERY + room, jnp.minimum(at, room - 1))


def add_terms(code, steps, total, blocks_of):
    def one(step, _):
        words = [code[0, step * STEP + k] for k in range(STEP)]
        terms = [product(*blocks_of(step * STEP + k, words[k])) for k in range(STEP)]
        for word, term in zip(words, terms):
            total[word % 8] += term
        return 0

    lax.fori_loop(0, steps, one, 0)


def fetch_kernel(code, info, panel, lefts, sems):
    many = (info[0, 0] + STEP - 1) // STEP * STEP

    def copy(t):
        return pltpu.make_async_copy(panel.at[(code[0, t] // 8) % 64], lefts.at[t], sems.at[t])

    def begin(t, _):
        copy(t).start()
        return 0

    def end(t, _):
        copy(t).wait()
        return 0

    lax.fori_loop(0, many, begin, 0)
    lax.fori_loop(0, many, end, 0)


def square_kernel(size, code, info, x, lefts, came, squared, spread, rights, total):
    local = x.shape[0]
    unpack(size, came, rights)
    rights[size:] = x[...]
    total[...] = jnp.zeros_like(total)

    def blocks_of(t, word):
        return lefts[t], rights[place(word // 65536, size)]

    add_terms(code, (info[0, 0] + STEP - 1) // STEP, total, blocks_of)
    squared[...] = total[:local]
    tall = spread.shape[2]
    for k in range(spread.shape[0]):
        spread[k] = squared[:, k * tall : (k + 1) * tall, :]


def cube_kernel(size, code, info, squared, came, rights, squared_out, purified_out, lefts, total, purified, sems):
    local = squared.shape[0]
    first = pltpu.make_async_copy(squared, squared_out, sems.at[0])
    first.start()
    unpack(size, came, lefts)
    lefts[size : size + local] = squared[...]
    total[...] = jnp.zeros_like(total)

    def blocks_of(t, word):
        return lefts[place((word // 512) % 128, size)], rights[place(word // 65536, size)]

    add_terms(code, (info[0, 0] + STEP - 1) // STEP, total, blocks_of)
    purified[...] = 3.0 * squared[...] - 2.0 * total[:local]
    second = pltpu.make_async_copy(purified, purified_out, sems.at[1])
    second.start()
    first.wait()
    second.wait()


def shape(*dims, dtype=F32):
    return jax.ShapeDtypeStruct(dims, dtype)


def deliver(size, axis, table, held):
    _, tall, order = held.shape
    out = pl.pallas_call(
        functools.partial(pack_kernel, size),
        out_shape=shape(lax.axis_size(axis), size, tall, order),
        in_specs=[SMEM, VMEM],
        out_specs=VMEM,
        compiler_params=PARAMS,
        name="pack",
    )(table, held)
    return lax.all_to_all(out, axis, 0, 0, tiled=True)


def branch(size, tables, code, info, x, both, held, alike):
    right, left = tables
    local, order, _ = x.shape
    groups = lax.axis_size("col")
    tall = order // groups
    panel = lax.all_gather(both, "col", axis=0, tiled=True, axis_index_groups=alike)
    came = deliver(size, "row", right, held)
    lefts = pl.pallas_call(
        fetch_kernel,
        out_shape=shape(size + local + 1, order, order),
        in_specs=[SMEM, SMEM, HBM],
        out_specs=VMEM,
        scratch_shapes=[pltpu.SemaphoreType.DMA((size + local + 1,))],
        compiler_params=PARAMS,
        name="fetch",
    )(code, info, panel)
    squared, spread, rights = pl.pallas_call(
        functools.partial(square_kernel, size),
        out_shape=(
            shape(local, order, order),
            shape(groups, local, tall, order),
            shape(size + local, order, order),
        ),
        in_specs=[SMEM, SMEM, VMEM, VMEM, VMEM],
        out_specs=(VMEM, VMEM, VMEM),
        scratch_shapes=[pltpu.VMEM((local + 1, order, order), F32)],
        compiler_params=PARAMS,
        name="square",
    )(code, info, x, lefts, came)
    held = lax.all_to_all(spread, "col", 0, 0, tiled=True)
    came = deliver(size, "col", left, held.reshape(groups * local, tall, order))
    return pl.pallas_call(
        functools.partial(cube_kernel, size),
        out_shape=(shape(local, order, order), shape(local, order, order)),
        in_specs=[SMEM, SMEM, VMEM, VMEM, VMEM],
        out_specs=(HBM, HBM),
        scratch_shapes=[
            pltpu.VMEM((size + local, order, order), F32),
            pltpu.VMEM((local + 1, order, order), F32),
            pltpu.VMEM((local, order, order), F32),
            pltpu.SemaphoreType.DMA((2,)),
        ],
        compiler_params=PARAMS,
        name="cube",
    )(code, info, squared, came, rights)


def body(density, columns):
    row_devs = lax.axis_size("row")
    rows, groups = columns.shape
    width = rows // groups
    local, _, order, _ = density.shape
    cand = local * groups
    fine, tall = order // row_devs, order // groups
    x = density[:, 0]
    spread = pl.pallas_call(
        spread_kernel,
        out_shape=shape(row_devs, local, fine, order),
        in_specs=[HBM],
        out_specs=HBM,
        scratch_shapes=[pltpu.SemaphoreType.DMA((local,))],
        compiler_params=PARAMS,
        name="spread",
    )(x.reshape(local, row_devs, fine, order))
    held = lax.all_to_all(spread, "row", 0, 0, tiled=True)
    held = held.reshape(row_devs * local, fine, order)
    here = jnp.stack([lax.axis_index("row"), lax.axis_index("col")]).astype(I32)
    cols = columns.astype(F32)
    right, left, code, info = pl.pallas_call(
        functools.partial(plan_kernel, rows, row_devs, groups, width),
        out_shape=(
            shape(cand, row_devs, dtype=I32),
            shape(cand, groups, dtype=I32),
            shape(1, 128, dtype=I32),
            shape(1, 128, dtype=I32),
        ),
        in_specs=[SMEM, VMEM, VMEM],
        out_specs=(VMEM, VMEM, VMEM, VMEM),
        compiler_params=PARAMS,
        name="plan",
    )(here, cols, cols.T)
    mate = lax.ppermute(x, "col", [(k, k ^ 2) for k in range(groups)])
    alike = [[k for k in range(groups) if (k // 2) % 2 == half] for half in range(2)]
    both = jnp.concatenate([x, mate])
    which, both, held = lax.optimization_barrier((info[0, 1], both, held))
    squared, purified = lax.switch(
        which,
        [functools.partial(branch, size, alike=alike) for size in SIZES],
        (right, left),
        code,
        info,
        x,
        both,
        held,
    )
    return squared[:, None], purified[:, None]


def solution(mesh):
    return jax.shard_map(
        body,
        mesh=mesh,
        in_specs=(P("row", "col", None, None), P()),
        out_specs=(P("row", "col", None, None), P("row", "col", None, None)),
        check_vma=False,
    )
```

```python
import functools

import jax
import jax.numpy as jnp
from jax import lax
from jax.experimental import pallas as pl
from jax.experimental.pallas import tpu as pltpu
from jax.sharding import PartitionSpec as P

F32 = jnp.float32
I32 = jnp.int32
VMEM = pl.BlockSpec(memory_space=pltpu.VMEM)
HBM = pl.BlockSpec(memory_space=pltpu.HBM)
SMEM = pl.BlockSpec(memory_space=pltpu.SMEM)
PARAMS = pltpu.CompilerParams(vmem_limit_bytes=24 << 20)
SIZES = (6, 7, 8, 9, 10, 11, 12, 13, 14, 16, 20, 64)
EVERY = SIZES[-1]
STEP = 4


def iota(shape, dim):
    return lax.broadcasted_iota(I32, shape, dim)


def eq(a, b):
    return (a == b).astype(F32)


def dot(a, b):
    return jnp.dot(a, b, preferred_element_type=F32)


def plan_kernel(rows, row_devs, groups, width, here, cols_ref, colst_ref, right_ref, left_ref, code_ref, info_ref):
    me, g_me = here[0], here[1]
    local = rows // row_devs
    cand = local * groups
    slots = cand
    cols = cols_ref[...]
    colst = colst_ref[...]
    s_j = eq(iota((rows, groups), 0) // width, iota((rows, groups), 1))
    j_s = eq(iota((groups, rows), 1) // width, iota((groups, rows), 0))
    mine_row = jnp.sum(jnp.where(iota((groups, rows), 0) == g_me, colst, 0.0), axis=0, keepdims=True)
    mine_col = jnp.sum(jnp.where(iota((rows, groups), 1) == g_me, cols, 0.0), axis=1, keepdims=True)
    by_source = dot(s_j, colst)
    term = (
        (by_source == (iota((rows, rows), 0) % width).astype(F32))
        & (mine_col == mine_row)
        & (mine_row >= 0)
    ).astype(F32)
    term = dot(j_s, term)
    source = iota((groups, rows), 0).astype(F32) * width + colst
    source = source.astype(I32)
    away = jnp.where((source // local) != (iota((groups, rows), 1) // local), term, 0.0)
    before = (iota((groups, groups), 1) < iota((groups, groups), 0)).astype(F32)
    count = jnp.sum(away, axis=0, keepdims=True)
    r0, r1 = iota((rows, rows), 0), iota((rows, rows), 1)
    earlier = ((r0 // local == r1 // local) & (r0 < r1)).astype(F32)
    rank = dot(before, away) + dot(jnp.broadcast_to(count, (8, rows)), earlier)[:1]
    rank = jnp.where(away > 0, rank, -1.0)
    slot = iota((slots, rows), 0).astype(F32)
    source_f = source.astype(F32)
    found = jnp.zeros((slots, rows), F32)
    for j in range(groups):
        found = found + jnp.where(rank[j : j + 1] == slot, source_f[j : j + 1], 0.0)
    fold = eq(iota((rows, row_devs), 0) // local, iota((rows, row_devs), 1))
    right_ref[...] = dot(found, fold).astype(I32)
    c0 = iota((cand, rows), 0)
    row_val = dot(eq(iota((cand, rows), 1), me * local + c0 // groups), cols)
    c1 = iota((cand, groups), 0)
    g1 = iota((cand, groups), 1)
    own = jnp.sum(jnp.where(g1 == c1 % groups, row_val, 0.0), axis=1, keepdims=True)
    q_1 = iota((cand, 1), 0) // groups
    j_1 = iota((cand, 1), 0) % groups
    s_1 = j_1 * width + own.astype(I32)
    s_val = dot(eq(iota((cand, rows), 1), s_1), cols)
    terms = ((own >= 0) & (row_val >= 0) & (s_val == row_val)).astype(F32)
    lefts = jnp.where(c1 % groups != g1, terms, 0.0)
    lower = (iota((cand, cand), 1) < iota((cand, cand), 0)).astype(F32)
    rank_l = dot(lower, lefts)
    marked = jnp.where(lefts > 0, rank_l, -1.0)
    piece = j_1 * local + q_1
    piece_f = piece.astype(F32)
    slot_g = iota((slots, groups), 0).astype(F32)
    got = jnp.zeros((slots, groups), F32)
    for k in range(cand):
        got = got + jnp.where(marked[k : k + 1] == slot_g, float((k % groups) * local + k // groups), 0.0)
    left_ref[...] = got.astype(I32)
    pick = g1 == g_me
    mine = jnp.sum(jnp.where(pick, terms, 0.0), axis=1, keepdims=True)
    l_rank = jnp.sum(jnp.where(pick, rank_l, 0.0), axis=1, keepdims=True)
    is_away = (s_1 // local != me).astype(F32)
    wide = iota((cand, 128), 1)
    both = jnp.where(wide == 0, mine, jnp.where(wide == 1, mine * is_away, 0.0))
    ranks = dot(lower, both)
    order = jnp.sum(jnp.where(wide == 0, ranks, 0.0), axis=1, keepdims=True)
    r_rank = jnp.sum(jnp.where(wide == 1, ranks, 0.0), axis=1, keepdims=True)
    l_at = jnp.where(j_1 == g_me, slots + q_1, l_rank.astype(I32))
    r_at = jnp.where(is_away > 0, r_rank.astype(I32), slots + s_1 % local)
    half = (j_1 // 2) % 2 != (g_me // 2) % 2
    panel_at = ((j_1 // 4) * 2 + j_1 % 2) * 2 + half.astype(I32)
    panel_at = panel_at * local + q_1
    code = (q_1 + 8 * panel_at + 512 * l_at + 65536 * r_at).astype(F32)
    idle = float(local + 512 * slots + 65536 * slots)
    hot = (mine > 0) & (order == wide.astype(F32))
    code = jnp.sum(jnp.where(hot, code - idle, 0.0), axis=0, keepdims=True) + idle
    code_ref[...] = code.astype(I32)
    values = rows // groups
    copy = eq(iota((groups, rows), 1) % groups, iota((groups, rows), 0))
    has = eq(dot(cols, copy), (iota((rows, rows), 1) // groups).astype(F32))
    filled = eq(dot(cols, j_s), (r1 % width).astype(F32))
    far = jnp.where(r0 // local != r1 // local, filled, 0.0)
    group_of = eq(iota((row_devs, rows), 1) // local, iota((row_devs, rows), 0))
    back = eq(iota((rows, groups), 0) % groups, iota((rows, groups), 1))
    need_r = dot(dot(group_of, dot(far, has) * has), back)
    need_l = dot(dot(group_of, (dot(filled, has) - 1.0) * has), back)
    number = jnp.sum(mine, axis=(0, 1), keepdims=True)
    most = jnp.max(jnp.maximum(need_r, need_l), axis=(0, 1), keepdims=True)
    which = sum((most > size).astype(F32) for size in SIZES[:-1])
    info_ref[...] = jnp.where(iota((1, 128), 1) == 0, number, which).astype(I32)


def pack_kernel(size, table, pieces, out, picks, sem):
    copy = pltpu.make_async_copy(table.at[: picks.shape[0]], picks, sem)
    copy.start()
    copy.wait()

    def one(step, _):
        for d in [step * 4 + k for k in range(4)]:
            for slot in range(size):
                out[d, slot] = pieces[picks[slot, d]]
        return 0

    lax.fori_loop(0, out.shape[0] // 4, one, 0)


def pack_out_kernel(size, table, pieces, out, picks, sem, buffer, sems):
    copy = pltpu.make_async_copy(table.at[: picks.shape[0]], picks, sem)
    copy.start()
    copy.wait()

    def leave(step):
        part = pl.ds(step * 4, 4)
        return pltpu.make_async_copy(buffer.at[part], out.at[part], sems.at[step])

    def one(step, _):
        for d in [step * 4 + k for k in range(4)]:
            for slot in range(size):
                buffer[d, slot] = pieces[picks[slot, d]]
        leave(step).start()
        return 0

    def end(step, _):
        leave(step).wait()
        return 0

    lax.fori_loop(0, out.shape[0] // 4, one, 0)
    lax.fori_loop(0, out.shape[0] // 4, end, 0)


def spread_kernel(x, out, blocks, buffer, in_sems, out_sems):
    enter = [pltpu.make_async_copy(x.at[b], blocks.at[b], in_sems.at[b]) for b in range(x.shape[0])]
    for copy in enter:
        copy.start()
    for copy in enter:
        copy.wait()
    many = out_sems.shape[0]
    wide = out.shape[0] // many
    leave = []
    for step in range(many):
        for d in range(step * wide, (step + 1) * wide):
            buffer[d] = blocks[:, d]
        part = pl.ds(step * wide, wide)
        leave.append(pltpu.make_async_copy(buffer.at[part], out.at[part], out_sems.at[step]))
        leave[-1].start()
    for copy in leave:
        copy.wait()


def halves(block):
    high = block.astype(jnp.bfloat16)
    return high, (block - high.astype(F32)).astype(jnp.bfloat16)


def product(left, right):
    lh, ll = halves(left)
    rh, rl = halves(right)
    return dot(jnp.concatenate([lh, lh, ll], axis=1), jnp.concatenate([rh, rl, rh], axis=0))


def unpack(size, came, blocks):
    tall = came.shape[2]

    def one(slot, _):
        for h in range(came.shape[0]):
            blocks[slot, h * tall : (h + 1) * tall, :] = came[h, slot]
        return 0

    lax.fori_loop(0, size, one, 0)


def place(at, room):
    return jnp.where(at >= EVERY, at - EVERY + room, jnp.minimum(at, room - 1))


def add_terms(code, steps, total, blocks_of):
    def one(step, _):
        words = [code[0, step * STEP + k] for k in range(STEP)]
        terms = [product(*blocks_of(step * STEP + k, words[k])) for k in range(STEP)]
        for word, term in zip(words, terms):
            total[word % 8] += term
        return 0

    lax.fori_loop(0, steps, one, 0)


def fetch_kernel(code, info, panel, lefts, sems):
    many = (info[0, 0] + STEP - 1) // STEP * STEP

    def copy(t):
        return pltpu.make_async_copy(panel.at[(code[0, t] // 8) % 64], lefts.at[t], sems.at[t])

    def begin(t, _):
        copy(t).start()
        return 0

    def end(t, _):
        copy(t).wait()
        return 0

    lax.fori_loop(0, many, begin, 0)
    lax.fori_loop(0, many, end, 0)


def square_kernel(size, code, info, x, lefts, came, squared, spread, rights, total):
    local = x.shape[0]
    unpack(size, came, rights)
    rights[size:] = x[...]
    total[...] = jnp.zeros_like(total)

    def blocks_of(t, word):
        return lefts[t], rights[place(word // 65536, size)]

    add_terms(code, (info[0, 0] + STEP - 1) // STEP, total, blocks_of)
    squared[...] = total[:local]
    tall = spread.shape[2]
    for k in range(spread.shape[0]):
        spread[k] = squared[:, k * tall : (k + 1) * tall, :]


def cube_kernel(size, code, info, squared, came, rights, squared_out, purified_out, lefts, total, purified, sems):
    local = squared.shape[0]
    first = pltpu.make_async_copy(squared, squared_out, sems.at[0])
    first.start()
    unpack(size, came, lefts)
    lefts[size : size + local] = squared[...]
    total[...] = jnp.zeros_like(total)

    def blocks_of(t, word):
        return lefts[place((word // 512) % 128, size)], rights[place(word // 65536, size)]

    add_terms(code, (info[0, 0] + STEP - 1) // STEP, total, blocks_of)
    purified[...] = 3.0 * squared[...] - 2.0 * total[:local]
    second = pltpu.make_async_copy(purified, purified_out, sems.at[1])
    second.start()
    first.wait()
    second.wait()


def shape(*dims, dtype=F32):
    return jax.ShapeDtypeStruct(dims, dtype)


def packed(size, axis, table, held):
    _, tall, order = held.shape
    many = lax.axis_size(axis)
    scratch = [
        pltpu.SMEM((-(-size // 8) * 8, table.shape[1]), I32),
        pltpu.SemaphoreType.DMA,
    ]
    early = axis == "row"
    if early:
        scratch += [
            pltpu.VMEM((many, size, tall, order), F32),
            pltpu.SemaphoreType.DMA((many // 4,)),
        ]
    out = pl.pallas_call(
        functools.partial(pack_out_kernel if early else pack_kernel, size),
        out_shape=shape(many, size, tall, order),
        in_specs=[VMEM, VMEM],
        out_specs=HBM if early else VMEM,
        scratch_shapes=scratch,
        compiler_params=PARAMS,
        name="pack",
    )(table, held)
    return out


def branch(size, tables, code, info, x, both, held, alike):
    right, left = tables
    local, order, _ = x.shape
    groups = lax.axis_size("col")
    tall = order // groups
    out = packed(size, "row", right, held)
    if size >= 10:
        both, out = lax.optimization_barrier((both, out))
    panel = lax.all_gather(both, "col", axis=0, tiled=True, axis_index_groups=alike)
    came = lax.all_to_all(out, "row", 0, 0, tiled=True)
    panel = pltpu.with_memory_space_constraint(panel, pltpu.HBM)
    lefts = pl.pallas_call(
        fetch_kernel,
        out_shape=shape(size + local + STEP - 1, order, order),
        in_specs=[SMEM, SMEM, HBM],
        out_specs=VMEM,
        scratch_shapes=[pltpu.SemaphoreType.DMA((size + local + STEP - 1,))],
        compiler_params=PARAMS,
        name="fetch",
    )(code, info, panel)
    squared, spread, rights = pl.pallas_call(
        functools.partial(square_kernel, size),
        out_shape=(
            shape(local, order, order),
            shape(groups, local, tall, order),
            shape(size + local, order, order),
        ),
        in_specs=[SMEM, SMEM, VMEM, VMEM, VMEM],
        out_specs=(VMEM, VMEM, VMEM),
        scratch_shapes=[pltpu.VMEM((local + 1, order, order), F32)],
        compiler_params=PARAMS,
        name="square",
    )(code, info, x, lefts, came)
    held = lax.all_to_all(spread, "col", 0, 0, tiled=True)
    out = packed(size, "col", left, held.reshape(groups * local, tall, order))
    came = lax.all_to_all(out, "col", 0, 0, tiled=True)
    return pl.pallas_call(
        functools.partial(cube_kernel, size),
        out_shape=(shape(local, order, order), shape(local, order, order)),
        in_specs=[SMEM, SMEM, VMEM, VMEM, VMEM],
        out_specs=(HBM, HBM),
        scratch_shapes=[
            pltpu.VMEM((size + local, order, order), F32),
            pltpu.VMEM((local + 1, order, order), F32),
            pltpu.VMEM((local, order, order), F32),
            pltpu.SemaphoreType.DMA((2,)),
        ],
        compiler_params=PARAMS,
        name="cube",
    )(code, info, squared, came, rights)


def body(density, columns):
    row_devs = lax.axis_size("row")
    rows, groups = columns.shape
    width = rows // groups
    local, _, order, _ = density.shape
    cand = local * groups
    fine, tall = order // row_devs, order // groups
    x = density[:, 0]
    spread = pl.pallas_call(
        spread_kernel,
        out_shape=shape(row_devs, local, fine, order),
        in_specs=[HBM],
        out_specs=HBM,
        scratch_shapes=[
            pltpu.VMEM((local, row_devs, fine, order), F32),
            pltpu.VMEM((row_devs, local, fine, order), F32),
            pltpu.SemaphoreType.DMA((local,)),
            pltpu.SemaphoreType.DMA((4,)),
        ],
        compiler_params=PARAMS,
        name="spread",
    )(x.reshape(local, row_devs, fine, order))
    held = lax.all_to_all(spread, "row", 0, 0, tiled=True)
    held = held.reshape(row_devs * local, fine, order)
    here = jnp.stack([lax.axis_index("row"), lax.axis_index("col")]).astype(I32)
    cols = columns.astype(F32)
    right, left, code, info = pl.pallas_call(
        functools.partial(plan_kernel, rows, row_devs, groups, width),
        out_shape=(
            shape(cand, row_devs, dtype=I32),
            shape(cand, groups, dtype=I32),
            shape(1, 128, dtype=I32),
            shape(1, 128, dtype=I32),
        ),
        in_specs=[SMEM, VMEM, VMEM],
        out_specs=(VMEM, VMEM, VMEM, VMEM),
        compiler_params=PARAMS,
        name="plan",
    )(here, cols, cols.T)
    mate = lax.ppermute(x, "col", [(k, k ^ 2) for k in range(groups)])
    alike = [[k for k in range(groups) if (k // 2) % 2 == half] for half in range(2)]
    both = jnp.concatenate([x, mate])
    which, both, held = lax.optimization_barrier((info[0, 1], both, held))
    squared, purified = lax.switch(
        which,
        [functools.partial(branch, size, alike=alike) for size in SIZES],
        (right, left),
        code,
        info,
        x,
        both,
        held,
    )
    return squared[:, None], purified[:, None]


def solution(mesh):
    return jax.shard_map(
        body,
        mesh=mesh,
        in_specs=(P("row", "col", None, None), P()),
        out_specs=(P("row", "col", None, None), P("row", "col", None, None)),
        check_vma=False,
    )
```

```python
import functools

import jax
import jax.numpy as jnp
from jax import lax
from jax.experimental import pallas as pl
from jax.experimental.pallas import tpu as pltpu
from jax.sharding import PartitionSpec as P

F32 = jnp.float32
I32 = jnp.int32
VMEM = pl.BlockSpec(memory_space=pltpu.VMEM)
ANY = pl.BlockSpec(memory_space=pl.ANY)
HBM = pl.BlockSpec(memory_space=pltpu.HBM)
SMEM = pl.BlockSpec(memory_space=pltpu.SMEM)
PARAMS = pltpu.CompilerParams(vmem_limit_bytes=24 << 20)
SIZES = (8, 9, 10, 11, 12, 14, 64)
EVERY = SIZES[-1]
STEP = 4


def iota(shape, dim):
    return lax.broadcasted_iota(I32, shape, dim)


def eq(a, b):
    return (a == b).astype(F32)


def dot(a, b):
    return jnp.dot(a, b, preferred_element_type=F32)


def plan_kernel(rows, row_devs, groups, width, here, cols_ref, colst_ref, right_ref, left_ref, code_ref, info_ref):
    me, g_me = here[0], here[1]
    local = rows // row_devs
    cand = local * groups
    slots = cand
    cols = cols_ref[...]
    colst = colst_ref[...]
    s_j = eq(iota((rows, groups), 0) // width, iota((rows, groups), 1))
    j_s = eq(iota((groups, rows), 1) // width, iota((groups, rows), 0))
    mine_row = jnp.sum(jnp.where(iota((groups, rows), 0) == g_me, colst, 0.0), axis=0, keepdims=True)
    mine_col = jnp.sum(jnp.where(iota((rows, groups), 1) == g_me, cols, 0.0), axis=1, keepdims=True)
    by_source = dot(s_j, colst)
    term = (
        (by_source == (iota((rows, rows), 0) % width).astype(F32))
        & (mine_col == mine_row)
        & (mine_row >= 0)
    ).astype(F32)
    term = dot(j_s, term)
    source = iota((groups, rows), 0).astype(F32) * width + colst
    source = source.astype(I32)
    away = jnp.where((source // local) != (iota((groups, rows), 1) // local), term, 0.0)
    before = (iota((groups, groups), 1) < iota((groups, groups), 0)).astype(F32)
    count = jnp.sum(away, axis=0, keepdims=True)
    r0, r1 = iota((rows, rows), 0), iota((rows, rows), 1)
    earlier = ((r0 // local == r1 // local) & (r0 < r1)).astype(F32)
    rank = dot(before, away) + dot(jnp.broadcast_to(count, (8, rows)), earlier)[:1]
    rank = jnp.where(away > 0, rank, -1.0)
    slot = iota((slots, rows), 0).astype(F32)
    source_f = source.astype(F32)
    found = jnp.zeros((slots, rows), F32)
    for j in range(groups):
        found = found + jnp.where(rank[j : j + 1] == slot, source_f[j : j + 1], 0.0)
    fold = eq(iota((rows, row_devs), 0) // local, iota((rows, row_devs), 1))
    right_ref[...] = dot(found, fold).astype(I32)
    c0 = iota((cand, rows), 0)
    row_val = dot(eq(iota((cand, rows), 1), me * local + c0 // groups), cols)
    c1 = iota((cand, groups), 0)
    g1 = iota((cand, groups), 1)
    own = jnp.sum(jnp.where(g1 == c1 % groups, row_val, 0.0), axis=1, keepdims=True)
    q_1 = iota((cand, 1), 0) // groups
    j_1 = iota((cand, 1), 0) % groups
    s_1 = j_1 * width + own.astype(I32)
    s_val = dot(eq(iota((cand, rows), 1), s_1), cols)
    terms = ((own >= 0) & (row_val >= 0) & (s_val == row_val)).astype(F32)
    lefts = jnp.where(c1 % groups != g1, terms, 0.0)
    lower = (iota((cand, cand), 1) < iota((cand, cand), 0)).astype(F32)
    rank_l = dot(lower, lefts)
    marked = jnp.where(lefts > 0, rank_l, -1.0)
    piece = j_1 * local + q_1
    piece_f = piece.astype(F32)
    slot_g = iota((slots, groups), 0).astype(F32)
    got = jnp.zeros((slots, groups), F32)
    for k in range(cand):
        got = got + jnp.where(marked[k : k + 1] == slot_g, float((k % groups) * local + k // groups), 0.0)
    left_ref[...] = got.astype(I32)
    pick = g1 == g_me
    mine = jnp.sum(jnp.where(pick, terms, 0.0), axis=1, keepdims=True)
    l_rank = jnp.sum(jnp.where(pick, rank_l, 0.0), axis=1, keepdims=True)
    is_away = (s_1 // local != me).astype(F32)
    wide = iota((cand, 128), 1)
    both = jnp.where(wide == 0, mine, jnp.where(wide == 1, mine * is_away, 0.0))
    ranks = dot(lower, both)
    order = jnp.sum(jnp.where(wide == 0, ranks, 0.0), axis=1, keepdims=True)
    r_rank = jnp.sum(jnp.where(wide == 1, ranks, 0.0), axis=1, keepdims=True)
    l_at = jnp.where(j_1 == g_me, slots + q_1, l_rank.astype(I32))
    r_at = jnp.where(is_away > 0, r_rank.astype(I32), slots + s_1 % local)
    other = ((j_1 + g_me) % 2).astype(I32)
    steps = (j_1 // 4 + 4 - g_me // 4) % 4
    half = (j_1 // 2 + g_me // 2) % 2
    panel_at = (other * 4 + steps) * 2 + half
    panel_at = panel_at * local + q_1
    code = (q_1 + 8 * panel_at + 512 * l_at + 65536 * r_at).astype(F32)
    idle = float(local + 512 * slots + 65536 * slots)
    hot = (mine > 0) & (order == wide.astype(F32))
    code = jnp.sum(jnp.where(hot, code - idle, 0.0), axis=0, keepdims=True) + idle
    code_ref[...] = code.astype(I32)
    values = rows // groups
    copy = eq(iota((groups, rows), 1) % groups, iota((groups, rows), 0))
    has = eq(dot(cols, copy), (iota((rows, rows), 1) // groups).astype(F32))
    filled = eq(dot(cols, j_s), (r1 % width).astype(F32))
    far = jnp.where(r0 // local != r1 // local, filled, 0.0)
    group_of = eq(iota((row_devs, rows), 1) // local, iota((row_devs, rows), 0))
    back = eq(iota((rows, groups), 0) % groups, iota((rows, groups), 1))
    need_r = dot(dot(group_of, dot(far, has) * has), back)
    need_l = dot(dot(group_of, (dot(filled, has) - 1.0) * has), back)
    number = jnp.sum(mine, axis=(0, 1), keepdims=True)
    most = jnp.max(jnp.maximum(need_r, need_l), axis=(0, 1), keepdims=True)
    which = sum((most > size).astype(F32) for size in SIZES[:-1])
    info_ref[...] = jnp.where(iota((1, 128), 1) == 0, number, which).astype(I32)


def pack_kernel(size, table, pieces, out, picks, sem):
    copy = pltpu.make_async_copy(table.at[: picks.shape[0]], picks, sem)
    copy.start()
    copy.wait()

    def one(step, _):
        for d in [step * 4 + k for k in range(4)]:
            for slot in range(size):
                out[d, slot] = pieces[picks[slot, d]]
        return 0

    lax.fori_loop(0, out.shape[0] // 4, one, 0)


def pack_out_kernel(size, table, pieces, out, picks, sem, buffer, sems):
    copy = pltpu.make_async_copy(table.at[: picks.shape[0]], picks, sem)
    copy.start()
    copy.wait()

    def leave(step):
        part = pl.ds(step * 4, 4)
        return pltpu.make_async_copy(buffer.at[part], out.at[part], sems.at[step])

    def one(step, _):
        for d in [step * 4 + k for k in range(4)]:
            for slot in range(size):
                buffer[d, slot] = pieces[picks[slot, d]]
        leave(step).start()
        return 0

    def end(step, _):
        leave(step).wait()
        return 0

    lax.fori_loop(0, out.shape[0] // 4, one, 0)
    lax.fori_loop(0, out.shape[0] // 4, end, 0)


def spread_kernel(x, out, blocks, buffer, in_sems, out_sems):
    enter = [pltpu.make_async_copy(x.at[b], blocks.at[b], in_sems.at[b]) for b in range(x.shape[0])]
    for copy in enter:
        copy.start()
    for copy in enter:
        copy.wait()
    many = out_sems.shape[0]
    wide = out.shape[0] // many
    leave = []
    for step in range(many):
        for d in range(step * wide, (step + 1) * wide):
            buffer[d] = blocks[:, d]
        part = pl.ds(step * wide, wide)
        leave.append(pltpu.make_async_copy(buffer.at[part], out.at[part], out_sems.at[step]))
        leave[-1].start()
    for copy in leave:
        copy.wait()


def halves(block):
    high = block.astype(jnp.bfloat16)
    return high, (block - high.astype(F32)).astype(jnp.bfloat16)


def product(left, right):
    lh, ll = halves(left)
    rh, rl = halves(right)
    return dot(jnp.concatenate([lh, lh, ll], axis=1), jnp.concatenate([rh, rl, rh], axis=0))


def unpack(size, came, blocks):
    tall = came.shape[2]

    def one(slot, _):
        for h in range(came.shape[0]):
            blocks[slot, h * tall : (h + 1) * tall, :] = came[h, slot]
        return 0

    lax.fori_loop(0, size, one, 0)


def place(at, room):
    return jnp.where(at >= EVERY, at - EVERY + room, jnp.minimum(at, room - 1))


def add_terms(code, steps, total, blocks_of):
    def one(step, _):
        words = [code[0, step * STEP + k] for k in range(STEP)]
        terms = [product(*blocks_of(step * STEP + k, words[k])) for k in range(STEP)]
        for word, term in zip(words, terms):
            total[word % 8] += term
        return 0

    lax.fori_loop(0, steps, one, 0)


def fetch_kernel(code, info, *refs):
    *sources, lefts, sems = refs
    many = (info[0, 0] + STEP - 1) // STEP * STEP
    local = sources[0].shape[0] // 2
    places = []
    for core in range(2):
        own, after, far_0, far_1, before = sources[core * 5 : core * 5 + 5]
        places += [(own, 0), (own, local), (after, 0), (after, local)]
        places += [(far_0, 0), (far_1, 0), (before, 0), (before, local)]

    def begin(t, _):
        at = (code[0, t] // 8) % 64
        for k, (source, first) in enumerate(places):

            @pl.when(at // local == k)
            def _():
                pltpu.make_async_copy(source.at[first + at % local], lefts.at[t], sems.at[t]).start()

        return 0

    def end(t, _):
        pltpu.make_async_copy(sources[0].at[0], lefts.at[t], sems.at[t]).wait()
        return 0

    lax.fori_loop(0, many, begin, 0)
    lax.fori_loop(0, many, end, 0)


def square_kernel(size, code, info, x, lefts, came, squared, spread, rights, total):
    local = x.shape[0]
    unpack(size, came, rights)
    rights[size:] = x[...]
    total[...] = jnp.zeros_like(total)

    def blocks_of(t, word):
        return lefts[t], rights[place(word // 65536, size)]

    add_terms(code, (info[0, 0] + STEP - 1) // STEP, total, blocks_of)
    squared[...] = total[:local]
    tall = spread.shape[2]
    for k in range(spread.shape[0]):
        spread[k] = squared[:, k * tall : (k + 1) * tall, :]


def cube_kernel(size, code, info, squared, came, rights, squared_out, purified_out, lefts, total, purified, sems):
    local = squared.shape[0]
    first = pltpu.make_async_copy(squared, squared_out, sems.at[0])
    first.start()
    unpack(size, came, lefts)
    lefts[size : size + local] = squared[...]
    total[...] = jnp.zeros_like(total)

    def blocks_of(t, word):
        return lefts[place((word // 512) % 128, size)], rights[place(word // 65536, size)]

    add_terms(code, (info[0, 0] + STEP - 1) // STEP, total, blocks_of)
    purified[...] = 3.0 * squared[...] - 2.0 * total[:local]
    second = pltpu.make_async_copy(purified, purified_out, sems.at[1])
    second.start()
    first.wait()
    second.wait()


def shape(*dims, dtype=F32):
    return jax.ShapeDtypeStruct(dims, dtype)


def packed(size, axis, table, held):
    _, tall, order = held.shape
    many = lax.axis_size(axis)
    scratch = [
        pltpu.SMEM((-(-size // 8) * 8, table.shape[1]), I32),
        pltpu.SemaphoreType.DMA,
    ]
    early = axis == "row"
    if early:
        scratch += [
            pltpu.VMEM((many, size, tall, order), F32),
            pltpu.SemaphoreType.DMA((many // 4,)),
        ]
    out = pl.pallas_call(
        functools.partial(pack_out_kernel if early else pack_kernel, size),
        out_shape=shape(many, size, tall, order),
        in_specs=[VMEM, VMEM],
        out_specs=HBM if early else VMEM,
        scratch_shapes=scratch,
        compiler_params=PARAMS,
        name="pack",
    )(table, held)
    return out


def branch(size, tables, code, info, x, both, held):
    right, left = tables
    local, order, _ = x.shape
    groups = lax.axis_size("col")
    tall = order // groups
    out = packed(size, "row", right, held)
    came = lax.all_to_all(out, "row", 0, 0, tiled=True)
    ring = range(groups)

    def along(block, by):
        return lax.ppermute(block, "col", [(k, (k + 4 * by) % groups) for k in ring])

    def across(block):
        return lax.ppermute(block, "col", [(k, k ^ 1) for k in ring])

    both, out = lax.optimization_barrier((both, out))
    before, after = along(both, 1), along(both, -1)
    far_0, far_1 = along(after[:local], -1), along(before[local:], 1)
    mine = (both, after, far_0, far_1, before)
    sources = (*mine, *[across(block) for block in mine])
    lefts = pl.pallas_call(
        fetch_kernel,
        out_shape=shape(size + local + STEP - 1, order, order),
        in_specs=[SMEM, SMEM, *[ANY] * len(sources)],
        out_specs=VMEM,
        scratch_shapes=[pltpu.SemaphoreType.DMA((size + local + STEP - 1,))],
        compiler_params=PARAMS,
        name="fetch",
    )(code, info, *sources)
    squared, spread, rights = pl.pallas_call(
        functools.partial(square_kernel, size),
        out_shape=(
            shape(local, order, order),
            shape(groups, local, tall, order),
            shape(size + local, order, order),
        ),
        in_specs=[SMEM, SMEM, VMEM, VMEM, VMEM],
        out_specs=(VMEM, VMEM, VMEM),
        scratch_shapes=[pltpu.VMEM((local + 1, order, order), F32)],
        compiler_params=PARAMS,
        name="square",
    )(code, info, x, lefts, came)
    held = lax.all_to_all(spread, "col", 0, 0, tiled=True)
    out = packed(size, "col", left, held.reshape(groups * local, tall, order))
    came = lax.all_to_all(out, "col", 0, 0, tiled=True)
    return pl.pallas_call(
        functools.partial(cube_kernel, size),
        out_shape=(shape(local, order, order), shape(local, order, order)),
        in_specs=[SMEM, SMEM, VMEM, VMEM, VMEM],
        out_specs=(HBM, HBM),
        scratch_shapes=[
            pltpu.VMEM((size + local, order, order), F32),
            pltpu.VMEM((local + 1, order, order), F32),
            pltpu.VMEM((local, order, order), F32),
            pltpu.SemaphoreType.DMA((2,)),
        ],
        compiler_params=PARAMS,
        name="cube",
    )(code, info, squared, came, rights)


def body(density, columns):
    row_devs = lax.axis_size("row")
    rows, groups = columns.shape
    width = rows // groups
    local, _, order, _ = density.shape
    cand = local * groups
    fine, tall = order // row_devs, order // groups
    x = density[:, 0]
    spread = pl.pallas_call(
        spread_kernel,
        out_shape=shape(row_devs, local, fine, order),
        in_specs=[HBM],
        out_specs=HBM,
        scratch_shapes=[
            pltpu.VMEM((local, row_devs, fine, order), F32),
            pltpu.VMEM((row_devs, local, fine, order), F32),
            pltpu.SemaphoreType.DMA((local,)),
            pltpu.SemaphoreType.DMA((4,)),
        ],
        compiler_params=PARAMS,
        name="spread",
    )(x.reshape(local, row_devs, fine, order))
    held = lax.all_to_all(spread, "row", 0, 0, tiled=True)
    held = held.reshape(row_devs * local, fine, order)
    here = jnp.stack([lax.axis_index("row"), lax.axis_index("col")]).astype(I32)
    cols = columns.astype(F32)
    right, left, code, info = pl.pallas_call(
        functools.partial(plan_kernel, rows, row_devs, groups, width),
        out_shape=(
            shape(cand, row_devs, dtype=I32),
            shape(cand, groups, dtype=I32),
            shape(1, 128, dtype=I32),
            shape(1, 128, dtype=I32),
        ),
        in_specs=[SMEM, VMEM, VMEM],
        out_specs=(VMEM, VMEM, VMEM, VMEM),
        compiler_params=PARAMS,
        name="plan",
    )(here, cols, cols.T)
    mate = lax.ppermute(x, "col", [(k, k ^ 2) for k in range(groups)])
    both = jnp.concatenate([x, mate])
    which, both, held = lax.optimization_barrier((info[0, 1], both, held))
    squared, purified = lax.switch(
        which,
        [functools.partial(branch, size) for size in SIZES],
        (right, left),
        code,
        info,
        x,
        both,
        held,
    )
    return squared[:, None], purified[:, None]


def solution(mesh):
    return jax.shard_map(
        body,
        mesh=mesh,
        in_specs=(P("row", "col", None, None), P()),
        out_specs=(P("row", "col", None, None), P("row", "col", None, None)),
        check_vma=False,
    )
```

```python
import functools

import jax
import jax.numpy as jnp
from jax import lax
from jax.experimental import pallas as pl
from jax.experimental.pallas import tpu as pltpu
from jax.sharding import PartitionSpec as P

F32 = jnp.float32
I32 = jnp.int32
VMEM = pl.BlockSpec(memory_space=pltpu.VMEM)
ANY = pl.BlockSpec(memory_space=pl.ANY)
HBM = pl.BlockSpec(memory_space=pltpu.HBM)
SMEM = pl.BlockSpec(memory_space=pltpu.SMEM)
PARAMS = pltpu.CompilerParams(vmem_limit_bytes=24 << 20)
SIZES = (8, 9, 10, 11, 12, 13, 14, 64)
EVERY = SIZES[-1]
STEP = 4


def iota(shape, dim):
    return lax.broadcasted_iota(I32, shape, dim)


def eq(a, b):
    return (a == b).astype(F32)


def dot(a, b):
    return jnp.dot(a, b, preferred_element_type=F32)


def plan_kernel(rows, row_devs, groups, width, here, cols_ref, colst_ref, right_ref, left_ref, code_ref, info_ref):
    me, g_me = here[0], here[1]
    local = rows // row_devs
    cand = local * groups
    slots = cand
    cols = cols_ref[...]
    colst = colst_ref[...]
    s_j = eq(iota((rows, groups), 0) // width, iota((rows, groups), 1))
    j_s = eq(iota((groups, rows), 1) // width, iota((groups, rows), 0))
    mine_row = jnp.sum(jnp.where(iota((groups, rows), 0) == g_me, colst, 0.0), axis=0, keepdims=True)
    mine_col = jnp.sum(jnp.where(iota((rows, groups), 1) == g_me, cols, 0.0), axis=1, keepdims=True)
    by_source = dot(s_j, colst)
    term = (
        (by_source == (iota((rows, rows), 0) % width).astype(F32))
        & (mine_col == mine_row)
        & (mine_row >= 0)
    ).astype(F32)
    term = dot(j_s, term)
    source = iota((groups, rows), 0).astype(F32) * width + colst
    source = source.astype(I32)
    away = jnp.where((source // local) != (iota((groups, rows), 1) // local), term, 0.0)
    before = (iota((groups, groups), 1) < iota((groups, groups), 0)).astype(F32)
    count = jnp.sum(away, axis=0, keepdims=True)
    r0, r1 = iota((rows, rows), 0), iota((rows, rows), 1)
    earlier = ((r0 // local == r1 // local) & (r0 < r1)).astype(F32)
    rank = dot(before, away) + dot(jnp.broadcast_to(count, (8, rows)), earlier)[:1]
    rank = jnp.where(away > 0, rank, -1.0)
    slot = iota((slots, rows), 0).astype(F32)
    source_f = source.astype(F32)
    found = jnp.zeros((slots, rows), F32)
    for j in range(groups):
        found = found + jnp.where(rank[j : j + 1] == slot, source_f[j : j + 1], 0.0)
    fold = eq(iota((rows, row_devs), 0) // local, iota((rows, row_devs), 1))
    right_ref[...] = dot(found, fold).astype(I32)
    c0 = iota((cand, rows), 0)
    row_val = dot(eq(iota((cand, rows), 1), me * local + c0 // groups), cols)
    c1 = iota((cand, groups), 0)
    g1 = iota((cand, groups), 1)
    own = jnp.sum(jnp.where(g1 == c1 % groups, row_val, 0.0), axis=1, keepdims=True)
    q_1 = iota((cand, 1), 0) // groups
    j_1 = iota((cand, 1), 0) % groups
    s_1 = j_1 * width + own.astype(I32)
    s_val = dot(eq(iota((cand, rows), 1), s_1), cols)
    terms = ((own >= 0) & (row_val >= 0) & (s_val == row_val)).astype(F32)
    lefts = jnp.where(c1 % groups != g1, terms, 0.0)
    lower = (iota((cand, cand), 1) < iota((cand, cand), 0)).astype(F32)
    rank_l = dot(lower, lefts)
    marked = jnp.where(lefts > 0, rank_l, -1.0)
    piece = j_1 * local + q_1
    piece_f = piece.astype(F32)
    slot_g = iota((slots, groups), 0).astype(F32)
    got = jnp.zeros((slots, groups), F32)
    for k in range(cand):
        got = got + jnp.where(marked[k : k + 1] == slot_g, float((k % groups) * local + k // groups), 0.0)
    left_ref[...] = got.astype(I32)
    pick = g1 == g_me
    mine = jnp.sum(jnp.where(pick, terms, 0.0), axis=1, keepdims=True)
    l_rank = jnp.sum(jnp.where(pick, rank_l, 0.0), axis=1, keepdims=True)
    is_away = (s_1 // local != me).astype(F32)
    wide = iota((cand, 128), 1)
    both = jnp.where(wide == 0, mine, jnp.where(wide == 1, mine * is_away, 0.0))
    ranks = dot(lower, both)
    order = jnp.sum(jnp.where(wide == 0, ranks, 0.0), axis=1, keepdims=True)
    r_rank = jnp.sum(jnp.where(wide == 1, ranks, 0.0), axis=1, keepdims=True)
    l_at = jnp.where(j_1 == g_me, slots + q_1, l_rank.astype(I32))
    r_at = jnp.where(is_away > 0, r_rank.astype(I32), slots + s_1 % local)
    other = ((j_1 + g_me) % 2).astype(I32)
    steps = (j_1 // 4 + 4 - g_me // 4) % 4
    half = (j_1 // 2 + g_me // 2) % 2
    panel_at = (other * 4 + steps) * 2 + half
    panel_at = panel_at * local + q_1
    code = (q_1 + 8 * panel_at + 512 * l_at + 65536 * r_at).astype(F32)
    idle = float(local + 512 * slots + 65536 * slots)
    hot = (mine > 0) & (order == wide.astype(F32))
    code = jnp.sum(jnp.where(hot, code - idle, 0.0), axis=0, keepdims=True) + idle
    code_ref[...] = code.astype(I32)
    values = rows // groups
    copy = eq(iota((groups, rows), 1) % groups, iota((groups, rows), 0))
    has = eq(dot(cols, copy), (iota((rows, rows), 1) // groups).astype(F32))
    filled = eq(dot(cols, j_s), (r1 % width).astype(F32))
    far = jnp.where(r0 // local != r1 // local, filled, 0.0)
    group_of = eq(iota((row_devs, rows), 1) // local, iota((row_devs, rows), 0))
    back = eq(iota((rows, groups), 0) % groups, iota((rows, groups), 1))
    need_r = dot(dot(group_of, dot(far, has) * has), back)
    need_l = dot(dot(group_of, (dot(filled, has) - 1.0) * has), back)
    number = jnp.sum(mine, axis=(0, 1), keepdims=True)
    most = jnp.max(jnp.maximum(need_r, need_l), axis=(0, 1), keepdims=True)
    which = sum((most > size).astype(F32) for size in SIZES[:-1])
    info_ref[...] = jnp.where(iota((1, 128), 1) == 0, number, which).astype(I32)


def pack_kernel(size, table, pieces, out, picks, sem):
    copy = pltpu.make_async_copy(table.at[: picks.shape[0]], picks, sem)
    copy.start()
    copy.wait()

    def one(step, _):
        for d in [step * 4 + k for k in range(4)]:
            for slot in range(size):
                out[d, slot] = pieces[picks[slot, d]]
        return 0

    lax.fori_loop(0, out.shape[0] // 4, one, 0)


def pack_out_kernel(size, table, pieces, out, picks, sem, buffer, sems):
    copy = pltpu.make_async_copy(table.at[: picks.shape[0]], picks, sem)
    copy.start()
    copy.wait()

    def leave(step):
        part = pl.ds(step * 4, 4)
        return pltpu.make_async_copy(buffer.at[part], out.at[part], sems.at[step])

    def one(step, _):
        for d in [step * 4 + k for k in range(4)]:
            for slot in range(size):
                buffer[d, slot] = pieces[picks[slot, d]]
        leave(step).start()
        return 0

    def end(step, _):
        leave(step).wait()
        return 0

    lax.fori_loop(0, out.shape[0] // 4, one, 0)
    lax.fori_loop(0, out.shape[0] // 4, end, 0)


def spread_kernel(x, out, blocks, buffer, in_sems, out_sems):
    enter = [pltpu.make_async_copy(x.at[b], blocks.at[b], in_sems.at[b]) for b in range(x.shape[0])]
    for copy in enter:
        copy.start()
    for b, copy in enumerate(enter):
        copy.wait()
        if b + 1 < len(enter):
            for d in range(out.shape[0]):
                buffer[d, b] = blocks[b, d]
    many = out_sems.shape[0]
    wide = out.shape[0] // many
    leave = []
    for step in range(many):
        for d in range(step * wide, (step + 1) * wide):
            buffer[d, x.shape[0] - 1] = blocks[x.shape[0] - 1, d]
        part = pl.ds(step * wide, wide)
        leave.append(pltpu.make_async_copy(buffer.at[part], out.at[part], out_sems.at[step]))
        leave[-1].start()
    for copy in leave:
        copy.wait()


def halves(block):
    high = block.astype(jnp.bfloat16)
    return high, (block - high.astype(F32)).astype(jnp.bfloat16)


def product(left, right):
    lh, ll = halves(left)
    rh, rl = halves(right)
    return dot(jnp.concatenate([lh, lh, ll], axis=1), jnp.concatenate([rh, rl, rh], axis=0))


def unpack(size, came, blocks):
    tall = came.shape[2]

    def one(slot, _):
        for h in range(came.shape[0]):
            blocks[slot, h * tall : (h + 1) * tall, :] = came[h, slot]
        return 0

    lax.fori_loop(0, size, one, 0)


def place(at, room):
    return jnp.where(at >= EVERY, at - EVERY + room, jnp.minimum(at, room - 1))


def add_terms(code, steps, total, blocks_of):
    def one(step, _):
        words = [code[0, step * STEP + k] for k in range(STEP)]
        terms = [product(*blocks_of(step * STEP + k, words[k])) for k in range(STEP)]
        for word, term in zip(words, terms):
            total[word % 8] += term
        return 0

    lax.fori_loop(0, steps, one, 0)


def fetch_kernel(code, info, *refs):
    *sources, lefts, sems = refs
    many = (info[0, 0] + STEP - 1) // STEP * STEP
    local = sources[0].shape[0] // 2
    places = []
    for core in range(2):
        own, after, far_0, far_1, before = sources[core * 5 : core * 5 + 5]
        places += [(own, 0), (own, local), (after, 0), (after, local)]
        places += [(far_0, 0), (far_1, 0), (before, 0), (before, local)]

    def begin(t, _):
        at = (code[0, t] // 8) % 64
        for k, (source, first) in enumerate(places):

            @pl.when(at // local == k)
            def _():
                pltpu.make_async_copy(source.at[first + at % local], lefts.at[t], sems.at[t]).start()

        return 0

    def end(t, _):
        pltpu.make_async_copy(sources[0].at[0], lefts.at[t], sems.at[t]).wait()
        return 0

    lax.fori_loop(0, many, begin, 0)
    lax.fori_loop(0, many, end, 0)


def square_kernel(size, code, info, x, lefts, came, squared, spread, rights, total):
    local = x.shape[0]
    unpack(size, came, rights)
    rights[size:] = x[...]
    total[...] = jnp.zeros_like(total)

    def blocks_of(t, word):
        return lefts[t], rights[place(word // 65536, size)]

    add_terms(code, (info[0, 0] + STEP - 1) // STEP, total, blocks_of)
    squared[...] = total[:local]
    tall = spread.shape[2]
    for k in range(spread.shape[0]):
        spread[k] = squared[:, k * tall : (k + 1) * tall, :]


def cube_kernel(size, code, info, squared, came, rights, squared_out, purified_out, lefts, total, purified, sems):
    local = squared.shape[0]
    first = pltpu.make_async_copy(squared, squared_out, sems.at[0])
    first.start()
    unpack(size, came, lefts)
    lefts[size : size + local] = squared[...]
    total[...] = jnp.zeros_like(total)

    def blocks_of(t, word):
        return lefts[place((word // 512) % 128, size)], rights[place(word // 65536, size)]

    add_terms(code, (info[0, 0] + STEP - 1) // STEP, total, blocks_of)
    leave = [pltpu.make_async_copy(purified.at[q], purified_out.at[q], sems.at[1 + q]) for q in range(local)]
    for q in range(local):
        purified[q] = 3.0 * squared[q] - 2.0 * total[q]
        leave[q].start()
    first.wait()
    for copy in leave:
        copy.wait()


def shape(*dims, dtype=F32):
    return jax.ShapeDtypeStruct(dims, dtype)


def packed(size, axis, table, held):
    _, tall, order = held.shape
    many = lax.axis_size(axis)
    scratch = [
        pltpu.SMEM((-(-size // 8) * 8, table.shape[1]), I32),
        pltpu.SemaphoreType.DMA,
    ]
    early = axis == "row"
    if early:
        scratch += [
            pltpu.VMEM((many, size, tall, order), F32),
            pltpu.SemaphoreType.DMA((many // 4,)),
        ]
    out = pl.pallas_call(
        functools.partial(pack_out_kernel if early else pack_kernel, size),
        out_shape=shape(many, size, tall, order),
        in_specs=[VMEM, VMEM],
        out_specs=HBM if early else VMEM,
        scratch_shapes=scratch,
        compiler_params=PARAMS,
        name="pack",
    )(table, held)
    return out


def branch(size, tables, code, info, x, both, held):
    right, left = tables
    local, order, _ = x.shape
    groups = lax.axis_size("col")
    tall = order // groups
    out = packed(size, "row", right, held)
    came = lax.all_to_all(out, "row", 0, 0, tiled=True)
    ring = range(groups)

    def along(block, by):
        return lax.ppermute(block, "col", [(k, (k + 4 * by) % groups) for k in ring])

    def across(block):
        return lax.ppermute(block, "col", [(k, k ^ 1) for k in ring])

    both, out = lax.optimization_barrier((both, out))
    before, after = along(both, 1), along(both, -1)
    far_0, far_1 = along(after[:local], -1), along(before[local:], 1)
    mine = (both, after, far_0, far_1, before)
    sources = (*mine, *[across(block) for block in mine])
    lefts = pl.pallas_call(
        fetch_kernel,
        out_shape=shape(size + local + STEP - 1, order, order),
        in_specs=[SMEM, SMEM, *[ANY] * len(sources)],
        out_specs=VMEM,
        scratch_shapes=[pltpu.SemaphoreType.DMA((size + local + STEP - 1,))],
        compiler_params=PARAMS,
        name="fetch",
    )(code, info, *sources)
    squared, spread, rights = pl.pallas_call(
        functools.partial(square_kernel, size),
        out_shape=(
            shape(local, order, order),
            shape(groups, local, tall, order),
            shape(size + local, order, order),
        ),
        in_specs=[SMEM, SMEM, VMEM, VMEM, VMEM],
        out_specs=(VMEM, VMEM, VMEM),
        scratch_shapes=[pltpu.VMEM((local + 1, order, order), F32)],
        compiler_params=PARAMS,
        name="square",
    )(code, info, x, lefts, came)
    held = lax.all_to_all(spread, "col", 0, 0, tiled=True)
    out = packed(size, "col", left, held.reshape(groups * local, tall, order))
    came = lax.all_to_all(out, "col", 0, 0, tiled=True)
    return pl.pallas_call(
        functools.partial(cube_kernel, size),
        out_shape=(shape(local, order, order), shape(local, order, order)),
        in_specs=[SMEM, SMEM, VMEM, VMEM, VMEM],
        out_specs=(HBM, HBM),
        scratch_shapes=[
            pltpu.VMEM((size + local, order, order), F32),
            pltpu.VMEM((local + 1, order, order), F32),
            pltpu.VMEM((local, order, order), F32),
            pltpu.SemaphoreType.DMA((1 + local,)),
        ],
        compiler_params=PARAMS,
        name="cube",
    )(code, info, squared, came, rights)


def body(density, columns):
    row_devs = lax.axis_size("row")
    rows, groups = columns.shape
    width = rows // groups
    local, _, order, _ = density.shape
    cand = local * groups
    fine, tall = order // row_devs, order // groups
    x = density[:, 0]
    spread = pl.pallas_call(
        spread_kernel,
        out_shape=shape(row_devs, local, fine, order),
        in_specs=[HBM],
        out_specs=HBM,
        scratch_shapes=[
            pltpu.VMEM((local, row_devs, fine, order), F32),
            pltpu.VMEM((row_devs, local, fine, order), F32),
            pltpu.SemaphoreType.DMA((local,)),
            pltpu.SemaphoreType.DMA((4,)),
        ],
        compiler_params=PARAMS,
        name="spread",
    )(x.reshape(local, row_devs, fine, order))
    held = lax.all_to_all(spread, "row", 0, 0, tiled=True)
    held = held.reshape(row_devs * local, fine, order)
    here = jnp.stack([lax.axis_index("row"), lax.axis_index("col")]).astype(I32)
    cols = columns.astype(F32)
    right, left, code, info = pl.pallas_call(
        functools.partial(plan_kernel, rows, row_devs, groups, width),
        out_shape=(
            shape(cand, row_devs, dtype=I32),
            shape(cand, groups, dtype=I32),
            shape(1, 128, dtype=I32),
            shape(1, 128, dtype=I32),
        ),
        in_specs=[SMEM, VMEM, VMEM],
        out_specs=(VMEM, VMEM, VMEM, VMEM),
        compiler_params=PARAMS,
        name="plan",
    )(here, cols, cols.T)
    mate = lax.ppermute(x, "col", [(k, k ^ 2) for k in range(groups)])
    both = jnp.concatenate([x, mate])
    which, both, held = lax.optimization_barrier((info[0, 1], both, held))
    squared, purified = lax.switch(
        which,
        [functools.partial(branch, size) for size in SIZES],
        (right, left),
        code,
        info,
        x,
        both,
        held,
    )
    return squared[:, None], purified[:, None]


def solution(mesh):
    return jax.shard_map(
        body,
        mesh=mesh,
        in_specs=(P("row", "col", None, None), P()),
        out_specs=(P("row", "col", None, None), P("row", "col", None, None)),
        check_vma=False,
    )
```
